256 devices in a mesh: row: 32 (over x, y, z_lo), col: 8 (over z_hi, core).
Axes of the slice: x: 4, y: 4, z: 8 (z_hi: 4, z_lo: 2; z = z_hi * 2 + z_lo), core: 2. Of those that a mesh axis runs over, the one named last changes fastest.
Arguments:
- features: float32 [65536, 256], P(('row', 'col')), may hold values from -6 to 6
- pre_act: float32 [65536, 256], P(('row', 'col')), may hold values from -6 to 6
- upstream: float32 [65536, 256], P(('row', 'col')), may hold values from -6 to 6
- weight: float32 [256, 256], replicated, may hold values from -0.375 to 0.375
- tile_vals: float32 [43520, 128, 128], P(('row', 'col')), may hold values from 0 to 0.046875
- tile_row: int32 [43520], P(('row', 'col')), may hold values from 0 to 15
- tile_col: int32 [43520], P(('row', 'col')), may hold values from 0 to 63
- tile_count: int32 [256], P(('row', 'col')), may hold values from 21 to 170, as said below
Outputs:
- grad_features: float32 [65536, 256], P(('row', 'col'))
- grad_weight: float32 [256, 256], replicated
The draws below stay inside these ranges and needn't reach their ends.
Inputs may be any that keep to these rules, and one draw needn't show every extreme that they name: `tile_count`: each device holds 170, // 2, // 4 or // 8 live tiles; some device holds exactly 170.
All inputs are finite; a program needn't handle non-finite values.
Results may differ from the reference program's by a relative error of at most 0.0003.
Values sent between devices are 32-bit elements; how exact they have to be, the bound alone decides.
A program may use at most 128 MiB of HBM per device.

```python
import math
import jax
import jax.numpy as jnp
from jax import lax

F = 256
TB = 128
NODES_DEV = 256
TILES_DEV = 170
NODES = 65536
N_ROW = 32
N_COL = 8
DEVICES = 256


def draw_tile_count(key, part):
    key = jax.random.fold_in(key, 7)
    first_key, second_key = jax.random.split(key)
    total = N_ROW * N_COL
    shifts = jax.random.randint(first_key, (total,), 0, 4)
    chosen = jax.random.randint(second_key, (), 0, total)
    shifts = jnp.where(jnp.arange(total) == chosen, 0, shifts)
    return (TILES_DEV // jnp.power(2, shifts)).astype(jnp.int32)


def set_ends(drawn, stream_key, low, largest):
    longest = drawn.shape.index(max(drawn.shape))
    spots = []
    for shift in (0, 1):
        where = [jax.random.randint(jax.random.fold_in(stream_key, axis), (), 0, length) for axis, length in enumerate(drawn.shape)]
        where[longest] = (where[longest] + shift) % drawn.shape[longest]
        spots.append(tuple(where))
    return drawn.at[spots[0]].set(low).at[spots[1]].set(largest)


def levels(key, dims, pieces, least, high):
    gain = 1.0
    for position, blocks in pieces:
        steps = jax.random.uniform(jax.random.fold_in(jax.random.fold_in(key, 6), position), (blocks,), jnp.float32, least / len(pieces), high / len(pieces))
        gain = gain * jnp.repeat(jnp.exp(steps), dims[position] // blocks).reshape((-1,) + (1,) * (len(dims) - 1 - position))
    return gain


def centred(key, shape, scale, reach, cuts=(), dtype=jnp.bfloat16):
    entries = scale * jax.random.normal(key, shape, jnp.float32)
    if cuts:
        entries = entries * levels(key, shape, cuts, -0.22, 0.18)
    return jnp.clip(entries, -reach, reach).astype(dtype)


def setup_inputs(seed: int = 0) -> dict:
    seeds = jax.random.split(jax.random.key(seed), 9)
    features = centred(seeds[0], (NODES, F), 1.0, 6.0, ((0, 256),), jnp.float32)
    pre_act = centred(seeds[1], (NODES, F), 1.5, 6.0, ((0, 256),), jnp.float32)
    upstream = centred(seeds[2], (NODES, F), 1.0, 6.0, ((0, 256),), jnp.float32)
    weight = centred(seeds[3], (F, F), F ** -0.5, 0.375, (), jnp.float32)
    tile_vals = jnp.clip(0.046875 * jax.random.uniform(seeds[4], (DEVICES * TILES_DEV, TB, TB), jnp.float32) ** levels(seeds[4], (DEVICES * TILES_DEV, TB, TB), ((0, 256),), -0.2, 0.2), 0.0, 0.046875)
    tile_row = set_ends(jax.random.randint(seeds[5], (DEVICES * TILES_DEV,), 0, NODES_DEV * N_COL // TB), jax.random.fold_in(seeds[5], 1), 0, (NODES_DEV * N_COL // TB) - 1).astype(jnp.int32)
    tile_col = set_ends(jax.random.randint(seeds[6], (DEVICES * TILES_DEV,), 0, NODES_DEV * N_ROW // TB), jax.random.fold_in(seeds[6], 1), 0, (NODES_DEV * N_ROW // TB) - 1).astype(jnp.int32)
    tile_count = draw_tile_count(jax.random.fold_in(seeds[8], 71), 0)
    return dict(features=features, pre_act=pre_act, upstream=upstream, weight=weight, tile_vals=tile_vals, tile_row=tile_row, tile_col=tile_col, tile_count=tile_count)


def reference(features, pre_act, upstream, weight, tile_vals, tile_row, tile_col, tile_count):
    gate_sig = jax.nn.sigmoid(pre_act)
    grad_pre = upstream * gate_sig * (1.0 + pre_act * (1.0 - gate_sig))
    row_tiles = NODES_DEV * N_COL // TB
    col_tiles = NODES_DEV * N_ROW // TB
    blocks = grad_pre.reshape(N_ROW, row_tiles, TB, F)
    values = tile_vals.reshape(N_ROW, N_COL, TILES_DEV, TB, TB)
    rows_all = tile_row.reshape(N_ROW, N_COL, TILES_DEV)
    cols_all = tile_col.reshape(N_ROW, N_COL, TILES_DEV)
    counts = tile_count.reshape(N_ROW, N_COL)

    def column_set(col_index):

        def add_row(row_index, total):
            picked = blocks[row_index][rows_all[row_index, col_index]]
            live_mask = (jnp.arange(TILES_DEV) < counts[row_index, col_index]).astype(jnp.float32)
            products = jnp.einsum('kab,kaf->kbf', values[row_index, col_index], picked, precision=lax.Precision.HIGHEST)
            products = products * live_mask[:, None, None]
            summed = jax.ops.segment_sum(products, cols_all[row_index, col_index], num_segments=col_tiles)
            return total + summed.reshape(col_tiles * TB, F)
        return lax.fori_loop(0, N_ROW, add_row, jnp.zeros((col_tiles * TB, F), jnp.float32))
    sets = lax.map(column_set, jnp.arange(N_COL))
    aggregated = sets.reshape(N_COL, N_ROW, NODES_DEV, F).transpose(1, 0, 2, 3).reshape(NODES, F)
    grad_features = jnp.dot(aggregated, weight.T, precision=lax.Precision.HIGHEST)
    grad_weight = jnp.dot(features.T, aggregated, precision=lax.Precision.HIGHEST) * (1.0 / math.sqrt(NODES))
    return (grad_features, grad_weight)
```

```python
import functools
import math

import jax
import jax.numpy as jnp
from jax import lax
from jax.experimental import pallas as pl
from jax.experimental.pallas import tpu as pltpu
from jax.sharding import PartitionSpec as P

MESH = pl.DeviceIdType.MESH
HIGH = lax.Precision.HIGHEST


def place():
    row = lax.axis_index("row")
    col = lax.axis_index("col")
    return row // 8, (row // 2) % 4, row % 2, col // 2, col % 2


def device(x, y, zl, zh, core):
    return (x * 8 + y * 2 + zl, zh * 2 + core)


def copy_to(src, dst, send, recv, target):
    return pltpu.make_async_remote_copy(
        src_ref=src, dst_ref=dst, send_sem=send, recv_sem=recv, device_id=target, device_id_type=MESH
    )


def greet(peers):
    barrier = pltpu.get_barrier_semaphore()
    for peer in peers:
        pl.semaphore_signal(barrier, inc=1, device_id=peer, device_id_type=MESH)
    pl.semaphore_wait(barrier, len(peers))


def gather_kernel(pre_ref, up_ref, gt_ref, send, recv):
    x, y, zl, zh, core = place()
    right = device(x, y, zl, (zh + 1) % 4, core)
    left = device(x, y, zl, (zh + 3) % 4, core)
    sibling = device(x, y, zl, zh, 1 - core)
    greet((right, left, sibling))
    pre = pre_ref[...]
    gate = jax.nn.sigmoid(pre)
    grad = up_ref[...] * gate * (1.0 + pre * (1.0 - gate))
    for t in range(2):
        gt_ref[zh * 4 + core * 2 + t] = grad[t * 128:(t + 1) * 128, :].T

    def part(block_zh, half):
        return gt_ref.at[pl.ds(block_zh * 4 + core * 2, 2), pl.ds(half * 128, 128), :]

    me, after, before, far = zh, (zh + 1) % 4, (zh + 3) % 4, (zh + 2) % 4
    started = []

    def go(ref, slot, target):
        copy = copy_to(ref, ref, send.at[slot], recv.at[slot], target)
        copy.start()
        started.append(copy)

    def arrived(ref, slot):
        copy_to(ref, ref, send.at[slot], recv.at[slot], right).wait_recv()

    go(part(me, 0), 0, right)
    go(part(me, 1), 3, left)
    go(part(me, 1), 1, right)
    go(part(me, 0), 2, left)
    go(part(me, 0), 6, sibling)
    go(part(me, 1), 7, sibling)
    arrived(part(before, 0), 0)
    go(part(before, 0), 4, right)
    arrived(part(after, 1), 3)
    go(part(after, 1), 5, left)
    go(part(before, 0), 8, sibling)
    go(part(after, 1), 9, sibling)
    arrived(part(before, 1), 1)
    go(part(before, 1), 10, sibling)
    arrived(part(after, 0), 2)
    go(part(after, 0), 11, sibling)
    arrived(part(far, 0), 4)
    go(part(far, 0), 12, sibling)
    arrived(part(far, 1), 5)
    go(part(far, 1), 13, sibling)
    other = 1 - core

    def mirrored(block_zh, half):
        return gt_ref.at[pl.ds(block_zh * 4 + other * 2, 2), pl.ds(half * 128, 128), :]

    for slot, (block, half) in zip(
        range(6, 14),
        ((me, 0), (me, 1), (before, 0), (after, 1), (before, 1), (after, 0), (far, 0), (far, 1)),
    ):
        arrived(mirrored(block, half), slot)
    for copy in started:
        copy.wait_send()


def gathered(pre_act, upstream):
    return pl.pallas_call(
        gather_kernel,
        out_shape=jax.ShapeDtypeStruct((16, 256, 128), jnp.float32),
        in_specs=[pl.BlockSpec(memory_space=pltpu.VMEM)] * 2,
        out_specs=pl.BlockSpec(memory_space=pltpu.VMEM),
        scratch_shapes=[pltpu.SemaphoreType.DMA((14,)), pltpu.SemaphoreType.DMA((14,))],
        compiler_params=pltpu.CompilerParams(collective_id=0, has_side_effects=True),
        name="gather",
    )(pre_act, upstream)


def split(value):
    high = value.astype(jnp.bfloat16)
    return high, (value - high.astype(jnp.float32)).astype(jnp.bfloat16)


STEP = 10


def tiles_kernel(rows, cols, count, gt_ref, tiles_ref, out_ref, parts):
    step = pl.program_id(0)

    @pl.when(step == 0)
    def _():
        @pl.loop(0, 64)
        def _(i):
            out_ref[i] = jnp.zeros((256, 128), jnp.float32)

        @pl.loop(0, 16)
        def _(i):
            high, low = split(gt_ref[i])
            parts[i, :, :128] = high
            parts[i, :, 128:] = low

    for j in range(STEP):
        k = step * STEP + j

        @pl.when(k < count[0])
        def _():
            high, low = split(tiles_ref[j])
            both = jnp.concatenate([high, low], axis=1)
            both = jnp.concatenate([both, both], axis=0)
            product = jnp.dot(parts[rows[k]], both, preferred_element_type=jnp.float32)
            out_ref[cols[k]] += product[:, :128] + product[:, 128:]


def tile_sums(tile_row, tile_col, tile_count, gt, tile_vals):
    slots = tile_vals.shape[0]
    return pl.pallas_call(
        tiles_kernel,
        out_shape=jax.ShapeDtypeStruct((64, 256, 128), jnp.float32),
        grid_spec=pltpu.PrefetchScalarGridSpec(
            num_scalar_prefetch=3,
            grid=(slots // STEP,),
            in_specs=[
                pl.BlockSpec(memory_space=pltpu.VMEM),
                pl.BlockSpec((STEP, 128, 128), lambda i, *_: (i, 0, 0)),
            ],
            out_specs=pl.BlockSpec(memory_space=pltpu.VMEM),
            scratch_shapes=[pltpu.VMEM((16, 256, 256), jnp.bfloat16)],
        ),
        compiler_params=pltpu.CompilerParams(vmem_limit_bytes=48 << 20),
        name="tiles",
    )(tile_row, tile_col, tile_count, gt, tile_vals)


def scatter_kernel(p_ref, agg_ref, r1, r2a, r2b, x1, s1, s2a, s2b, x2, zbuf, *sems):
    x, y, zl, zh, core = place()
    (r1s, r1r, r2as, r2ar, r2bs, r2br, s1s, s1r, s2as, s2ar, s2bs, s2br, zs, zr) = sems
    x_side = (device((x + 1) % 4, y, zl, zh, core), device((x + 3) % 4, y, zl, zh, core))
    y_side = (device(x, (y + 1) % 4, zl, zh, core), device(x, (y + 3) % 4, zl, zh, core))
    z_side = device(x, y, 1 - zl, zh, core)
    greet(x_side + y_side + (z_side,))
    first = (x_side, y_side)
    second = (y_side, x_side)
    c1 = (x, y)
    c2 = (y, x)
    order = (2, 1, 3, 0)
    sides = tuple((h, d) for h in range(2) for d in range(2))
    ahead = (1, 3)

    def block(h, d1, p, q):
        d1 = (c1[h] + d1) % 4
        d2 = (c2[h] + order[p]) % 4
        rows = pl.ds(h * 128 + q * 64, 64)
        return p_ref.at[d1, d2, :, rows, :] if h == 0 else p_ref.at[d2, d1, :, rows, :]

    started = []

    def go(src, dst, send, recv, target):
        copy = copy_to(src, dst, send, recv, target)
        copy.start()
        started.append(copy)
        return copy

    def arrived(dst, send, recv):
        copy_to(dst, dst, send, recv, z_side).wait_recv()

    for p in range(4):
        for h, d in sides:
            go(block(h, 2, p, d), r1.at[h, d, p], r1s.at[h, d, p], r1r.at[h, d, p], first[h][d])
    for p in range(4):
        for h, d in sides:
            arrived(r1.at[h, d, p], r1s.at[h, d, p], r1r.at[h, d, p])
            r1[h, d, p] += block(h, ahead[d], p, d)[...]
            go(r1.at[h, d, p], r2b.at[h, d, p], r2bs.at[h, d, p], r2br.at[h, d, p], first[h][d])
            go(block(h, ahead[d], p, 1 - d), r2a.at[h, d, p], r2as.at[h, d, p], r2ar.at[h, d, p], first[h][d])
    for p in range(4):
        for h in range(2):
            for d in range(2):
                arrived(r2a.at[h, d, p], r2as.at[h, d, p], r2ar.at[h, d, p])
                arrived(r2b.at[h, d, p], r2bs.at[h, d, p], r2br.at[h, d, p])
            for q in range(2):
                x1[h, p, q] = block(h, 0, p, q)[...] + r2b[h, q, p] + r2a[h, 1 - q, p]
            if p == 0:
                for d in range(2):
                    go(x1.at[h, 0, d], s1.at[h, d], s1s.at[h, d], s1r.at[h, d], second[h][d])
            elif p < 3:
                d = p - 1
                go(x1.at[h, p, 1 - d], s2a.at[h, d], s2as.at[h, d], s2ar.at[h, d], second[h][d])
                arrived(s1.at[h, d], s1s.at[h, d], s1r.at[h, d])
                x1[h, p, d] += s1[h, d]
                go(x1.at[h, p, d], s2b.at[h, d], s2bs.at[h, d], s2br.at[h, d], second[h][d])
    for h in range(2):
        for d in range(2):
            arrived(s2a.at[h, d], s2as.at[h, d], s2ar.at[h, d])
            arrived(s2b.at[h, d], s2bs.at[h, d], s2br.at[h, d])
        for q in range(2):
            x2[h, q] = x1[h, 3, q] + s2b[h, q] + s2a[h, 1 - q]
        go(x2.at[h, :, pl.ds(2 - 2 * zl, 2)], zbuf.at[h], zs.at[h], zr.at[h], z_side)
    for h in range(2):
        arrived(zbuf.at[h], zs.at[h], zr.at[h])
        for q in range(2):
            agg_ref[:, h * 128 + q * 64:h * 128 + q * 64 + 64, :] = (
                x2[h, q, pl.ds(2 * zl, 2)] + zbuf[h, q]
            )
    for copy in started:
        copy.wait_send()


def scattered(partial_sums):
    piece = (4, 64, 128)
    f32 = jnp.float32
    dma = pltpu.SemaphoreType.DMA
    return pl.pallas_call(
        scatter_kernel,
        out_shape=jax.ShapeDtypeStruct((2, 256, 128), f32),
        in_specs=[pl.BlockSpec(memory_space=pltpu.VMEM)],
        out_specs=pl.BlockSpec(memory_space=pltpu.VMEM),
        scratch_shapes=[
            pltpu.VMEM((2, 2, 4) + piece, f32),
            pltpu.VMEM((2, 2, 4) + piece, f32),
            pltpu.VMEM((2, 2, 4) + piece, f32),
            pltpu.VMEM((2, 4, 2) + piece, f32),
            pltpu.VMEM((2, 2) + piece, f32),
            pltpu.VMEM((2, 2) + piece, f32),
            pltpu.VMEM((2, 2) + piece, f32),
            pltpu.VMEM((2, 2) + piece, f32),
            pltpu.VMEM((2, 2, 2, 64, 128), f32),
        ]
        + [dma((2, 2, 4))] * 6
        + [dma((2, 2))] * 6
        + [dma((2,))] * 2,
        compiler_params=pltpu.CompilerParams(
            collective_id=1, has_side_effects=True, vmem_limit_bytes=48 << 20
        ),
        name="scatter",
    )(partial_sums.reshape(4, 4, 4, 256, 128))


def finish_kernel(agg_ref, feat_ref, weight_ref, gf_ref, gw_ref, local, a1, part, a2, whole, s1, r1, s2, r2, s3, r3):
    x, y, zl, zh, core = place()
    me = x * 8 + y * 2 + core
    mz = zh * 2 + zl

    def plane(j):
        return device(j // 8, (j // 2) % 4, zl, zh, j % 2)

    def column(j):
        return device(x, y, j % 2, j // 2, core)

    barrier = pltpu.get_barrier_semaphore()

    @pl.loop(1, 32)
    def _(j):
        pl.semaphore_signal(barrier, inc=1, device_id=plane((me + j) % 32), device_id_type=MESH)

    @pl.loop(1, 8)
    def _(j):
        pl.semaphore_signal(barrier, inc=1, device_id=column((mz + j) % 8), device_id_type=MESH)

    grad = jnp.dot(agg_ref[0], feat_ref[:128], precision=HIGH, preferred_element_type=jnp.float32)
    grad += jnp.dot(agg_ref[1], feat_ref[128:], precision=HIGH, preferred_element_type=jnp.float32)
    local[...] = grad.reshape(32, 8, 256)
    pl.semaphore_wait(barrier, 38)

    @pl.loop(1, 32)
    def _(j):
        to = (me + j) % 32
        copy_to(local.at[to], a1.at[me], s1, r1, plane(to)).start()

    a1[me] = local[me]
    for t in range(2):
        gf_ref[:, t * 128:(t + 1) * 128] = jnp.dot(
            weight_ref[...], agg_ref[t], precision=HIGH, preferred_element_type=jnp.float32
        )
    all_but_one = pltpu.make_async_copy(a1.at[pl.ds(0, 31)], a1.at[pl.ds(0, 31)], r1)
    all_but_one.wait()
    part[...] = jnp.sum(a1[...], axis=0)

    @pl.loop(1, 8)
    def _(j):
        copy_to(part, a2.at[mz], s2, r2, column((mz + j) % 8)).start()

    a2[mz] = part[...]
    pltpu.make_async_copy(a2.at[pl.ds(0, 7)], a2.at[pl.ds(0, 7)], r2).wait()
    whole[me] = jnp.sum(a2[...], axis=0)

    @pl.loop(1, 32)
    def _(j):
        copy_to(whole.at[me], whole.at[me], s3, r3, plane((me + j) % 32)).start()

    pltpu.make_async_copy(whole.at[pl.ds(0, 31)], whole.at[pl.ds(0, 31)], r3).wait()
    gw_ref[...] = whole[...].reshape(256, 256)
    pltpu.make_async_copy(a1.at[pl.ds(0, 31)], a1.at[pl.ds(0, 31)], s1).wait()
    pltpu.make_async_copy(a2.at[pl.ds(0, 7)], a2.at[pl.ds(0, 7)], s2).wait()
    pltpu.make_async_copy(whole.at[pl.ds(0, 31)], whole.at[pl.ds(0, 31)], s3).wait()


def finished(agg, features, weight):
    f32 = jnp.float32
    dma = pltpu.SemaphoreType.DMA
    square = jax.ShapeDtypeStruct((256, 256), f32)
    return pl.pallas_call(
        finish_kernel,
        out_shape=(square, square),
        in_specs=[pl.BlockSpec(memory_space=pltpu.VMEM)] * 3,
        out_specs=(pl.BlockSpec(memory_space=pltpu.VMEM),) * 2,
        scratch_shapes=[
            pltpu.VMEM((32, 8, 256), f32),
            pltpu.VMEM((32, 8, 256), f32),
            pltpu.VMEM((8, 256), f32),
            pltpu.VMEM((8, 8, 256), f32),
            pltpu.VMEM((32, 8, 256), f32),
        ]
        + [dma] * 6,
        compiler_params=pltpu.CompilerParams(collective_id=2, has_side_effects=True),
        name="finish",
    )(agg, features, weight)


def on_device(features, pre_act, upstream, weight, tile_vals, tile_row, tile_col, tile_count):
    gt = gathered(pre_act, upstream)
    sums = tile_sums(tile_row, tile_col, tile_count, gt, tile_vals)
    agg = scattered(sums)
    gf, gw = finished(agg, features, weight)
    total_nodes = features.shape[0] * 256
    return gf.T, gw.T * (1.0 / math.sqrt(total_nodes))


def solution(mesh):
    return jax.shard_map(
        on_device,
        mesh=mesh,
        in_specs=(
            P(("row", "col"), None),
            P(("row", "col"), None),
            P(("row", "col"), None),
            P(),
            P(("row", "col"), None, None),
            P(("row", "col")),
            P(("row", "col")),
            P(("row", "col")),
        ),
        out_specs=(P(("row", "col"), None), P()),
        check_vma=False,
    )
```

```python
import math

import jax
import jax.numpy as jnp
from jax import lax
from jax.experimental import pallas as pl
from jax.experimental.pallas import tpu as pltpu
from jax.sharding import PartitionSpec as P

MESH = pl.DeviceIdType.MESH
HIGH = lax.Precision.HIGHEST
F32 = jnp.float32
BF16 = jnp.bfloat16
SLOTS = 170
UNROLL = 34
LOADS = 10


def place():
    row = lax.axis_index("row")
    col = lax.axis_index("col")
    return row // 8, (row // 2) % 4, row % 2, col // 2, col % 2


def device(x, y, zl, zh, core):
    return (x * 8 + y * 2 + zl, zh * 2 + core)


def copy_to(src, dst, send, recv, target):
    return pltpu.make_async_remote_copy(
        src_ref=src, dst_ref=dst, send_sem=send, recv_sem=recv, device_id=target, device_id_type=MESH
    )


def split(value):
    high = value.astype(BF16)
    return high, (value - high.astype(F32)).astype(BF16)


def dot(a, b):
    return jnp.dot(a, b, precision=HIGH, preferred_element_type=F32)


def kernel(
    pre_ref, up_ref, feat_ref, weight_ref, row_ref, col_ref, count_ref, tiles_hbm,
    gf_ref, gw_ref,
    tiles, runs, parts, gt, sums, r1, r2a, r2b, x1, s1, s2a, s2b, x2, zbuf, agg, local, a1, part, a2,
    raw, table_v, table,
    load_sem, table_sem, ag_s, ag_r, r1s, r1r, r2as, r2ar, r2bs, r2br, s1s, s1r, s2as, s2ar, s2bs, s2br, zs, zr,
    w1s, w1r, w2s, w2r, w3s, w3r,
):
    x, y, zl, zh, core = place()
    me = x * 8 + y * 2 + core
    mz = zh * 2 + zl
    here = zh * 4 + core * 2

    def plane(j):
        return device(j // 8, (j // 2) % 4, zl, zh, j % 2)

    def column(j):
        return device(x, y, j % 2, j // 2, core)

    barrier = pltpu.get_barrier_semaphore()

    @pl.loop(1, 32)
    def _(j):
        pl.semaphore_signal(barrier, inc=1, device_id=plane((me + j) % 32), device_id_type=MESH)

    @pl.loop(1, 8)
    def _(j):
        pl.semaphore_signal(barrier, inc=1, device_id=column((mz + j) % 8), device_id_type=MESH)

    per_load = SLOTS // LOADS
    loads = []
    for i in range(LOADS):
        rows = pl.ds(i * per_load, per_load)
        loads.append(pltpu.make_async_copy(tiles_hbm.at[rows], tiles.at[rows], load_sem.at[i]))
        loads[-1].start()

    pre = pre_ref[...]
    gate = jax.nn.sigmoid(pre)
    grad = up_ref[...] * gate * (1.0 + pre * (1.0 - gate))
    for t in range(2):
        turned = grad[t * 128:(t + 1) * 128, :].T
        for h in range(2):
            gt[h, here + t] = turned[h * 128:(h + 1) * 128]
    pl.semaphore_wait(barrier, 38)

    started = []

    def go(src, dst, send, recv, target):
        copy = copy_to(src, dst, send, recv, target)
        copy.start()
        started.append(copy)

    z_right = device(x, y, zl, (zh + 1) % 4, core)
    z_left = device(x, y, zl, (zh + 3) % 4, core)
    sibling = device(x, y, zl, zh, 1 - core)
    z_side = device(x, y, 1 - zl, zh, core)
    x_side = (device((x + 1) % 4, y, zl, zh, core), device((x + 3) % 4, y, zl, zh, core))
    y_side = (device(x, (y + 1) % 4, zl, zh, core), device(x, (y + 3) % 4, zl, zh, core))

    def arrived(dst, send, recv):
        copy_to(dst, dst, send, recv, z_side).wait_recv()

    after, before, far = (zh + 1) % 4, (zh + 3) % 4, (zh + 2) % 4

    def block(h, block_zh, block_core, quarter):
        return gt.at[h, pl.ds(block_zh * 4 + block_core * 2, 2), pl.ds(quarter * 64, 64), :]

    def pass_on(h, block_zh, quarter, slot, target):
        ref = block(h, block_zh, core, quarter)
        go(ref, ref, ag_s.at[h, slot], ag_r.at[h, slot], target)

    def came(h, block_zh, block_core, quarter, slot):
        arrived(block(h, block_zh, block_core, quarter), ag_s.at[h, slot], ag_r.at[h, slot])

    def gather_own(h):
        pass_on(h, zh, 0, 0, z_right)
        pass_on(h, zh, 1, 3, z_left)
        pass_on(h, zh, 1, 1, z_right)
        pass_on(h, zh, 0, 2, z_left)
        pass_on(h, zh, 0, 6, sibling)
        pass_on(h, zh, 1, 7, sibling)

    def gather_next(h):
        came(h, before, core, 0, 0)
        pass_on(h, before, 0, 4, z_right)
        came(h, after, core, 1, 3)
        pass_on(h, after, 1, 5, z_left)
        pass_on(h, before, 0, 8, sibling)
        pass_on(h, after, 1, 9, sibling)
        came(h, before, core, 1, 1)
        pass_on(h, before, 1, 10, sibling)
        came(h, after, core, 0, 2)
        pass_on(h, after, 0, 11, sibling)

    def gather_last(h):
        came(h, far, core, 0, 4)
        pass_on(h, far, 0, 12, sibling)
        came(h, far, core, 1, 5)
        pass_on(h, far, 1, 13, sibling)
        blocks = ((zh, 0), (zh, 1), (before, 0), (after, 1), (before, 1), (after, 0), (far, 0), (far, 1))
        for i, (block_zh, quarter) in enumerate(blocks):
            came(h, block_zh, 1 - core, quarter, 6 + i)

    def sort_tiles():
        raw[...] = jnp.zeros((8, 256), jnp.int32)
        raw[0:1, 0:SLOTS] = col_ref[...]
        raw[1:2, 0:SLOTS] = row_ref[...]
        lane = lax.broadcasted_iota(jnp.int32, (8, 256), 1)
        across = lax.broadcasted_iota(jnp.int32, (256, 256), 1)
        slot_down = lax.broadcasted_iota(jnp.int32, (256, 1), 0)
        one, none = jnp.int32(1), jnp.int32(0)

        def down(value):
            return jnp.broadcast_to(value, (8, 256)).T[:, 0:1]

        def total(value):
            return jnp.sum(value, axis=0, keepdims=True)

        def within(value, last):
            return jnp.minimum(jnp.maximum(value, 0), last)

        values = raw[...]
        cols = jnp.where(lane < count_ref[0], values[0:1], 64)
        key = cols * 256 + lane
        rank = down(total(jnp.where(down(key[0:1]) < key[0:1], one, none)))
        col_down, row_down = down(cols[0:1]), down(values[1:2])
        at = rank == across
        next_at = rank + 1 == across
        sorted_cols = total(jnp.where(at, col_down, 0))
        previous = total(jnp.where(next_at, col_down + 1, 0)) - 1
        table_v[0:1] = within(total(jnp.where(at, slot_down, 0)), SLOTS - 1)
        table_v[1:2] = within(total(jnp.where(at, row_down, 0)), 15)
        table_v[2:3] = jnp.where(sorted_cols == previous, one, none)
        table_v[3:4] = within(total(jnp.where(col_down <= across, one, none)), SLOTS)
        table_v[4:5] = jnp.where(total(jnp.where(col_down == across, one, none)) > 0, one, none)
        table_v[5:8] = jnp.zeros((3, 256), jnp.int32)
        copy = pltpu.make_async_copy(table_v, table, table_sem)
        copy.start()
        copy.wait()

    def products(h):
        @pl.loop(0, 16)
        def _(i):
            high, low = split(gt[h, i])
            parts[i, :, :128] = high
            parts[i, :, 128:] = low

        @pl.loop(0, SLOTS // UNROLL)
        def _(i):
            for j in range(UNROLL):
                k = i * UNROLL + j
                high, low = split(tiles[table[0, k]])
                both = jnp.concatenate([high, low], axis=1)
                both = jnp.concatenate([both, both], axis=0)
                product = jnp.dot(parts[table[1, k]], both, preferred_element_type=F32)
                carried = table[2, k].astype(F32) * runs[k]
                runs[k + 1] = carried + product[:, :128] + product[:, 128:]

        @pl.loop(0, 16)
        def _(i):
            for j in range(4):
                t = i * 4 + j
                sums[h, i // 4, i % 4, j] = table[4, t].astype(F32) * runs[table[3, t]]

    first, second = (x_side, y_side), (y_side, x_side)
    c1, c2 = (x, y), (y, x)
    order = (2, 1, 3, 0)
    ahead = (1, 3)
    sides = tuple((a, d) for a in range(2) for d in range(2))

    def piece(h, a, d1, p, q):
        d1 = (c1[a] + d1) % 4
        d2 = (c2[a] + order[p]) % 4
        rows = pl.ds(a * 64 + q * 32, 32)
        return sums.at[h, d1, d2, :, rows, :] if a == 0 else sums.at[h, d2, d1, :, rows, :]

    def scatter_start(h):
        for p in range(4):
            for a, d in sides:
                i = (h, a, d, p)
                go(piece(h, a, 2, p, d), r1.at[i], r1s.at[i], r1r.at[i], first[a][d])

    def scatter_direct(h):
        for p in range(4):
            for a, d in sides:
                i = (h, a, d, p)
                go(piece(h, a, ahead[d], p, 1 - d), r2a.at[i], r2as.at[i], r2ar.at[i], first[a][d])

    def scatter_ring(h):
        for p in range(4):
            for a, d in sides:
                i = (h, a, d, p)
                arrived(r1.at[i], r1s.at[i], r1r.at[i])
                r1[i] += piece(h, a, ahead[d], p, d)[...]
                go(r1.at[i], r2b.at[i], r2bs.at[i], r2br.at[i], first[a][d])

    def scatter_cross(h, p):
        for a in range(2):
            for d in range(2):
                i = (h, a, d, p)
                arrived(r2a.at[i], r2as.at[i], r2ar.at[i])
                arrived(r2b.at[i], r2bs.at[i], r2br.at[i])
            for q in range(2):
                x1[h, a, p, q] = piece(h, a, 0, p, q)[...] + r2b[h, a, q, p] + r2a[h, a, 1 - q, p]
            if p == 0:
                for d in range(2):
                    i = (h, a, d)
                    go(x1.at[h, a, 0, d], s1.at[i], s1s.at[i], s1r.at[i], second[a][d])
            elif p < 3:
                i = (h, a, p - 1)
                go(x1.at[h, a, p, 2 - p], s2a.at[i], s2as.at[i], s2ar.at[i], second[a][p - 1])

    def scatter_cross_ring(h):
        for p in (1, 2):
            for a in range(2):
                i = (h, a, p - 1)
                arrived(s1.at[i], s1s.at[i], s1r.at[i])
                x1[h, a, p, p - 1] += s1[i]
                go(x1.at[h, a, p, p - 1], s2b.at[i], s2bs.at[i], s2br.at[i], second[a][p - 1])

    def scatter_z(h):
        for a in range(2):
            for d in range(2):
                i = (h, a, d)
                arrived(s2a.at[i], s2as.at[i], s2ar.at[i])
                arrived(s2b.at[i], s2bs.at[i], s2br.at[i])
            for q in range(2):
                x2[h, a, q] = x1[h, a, 3, q] + s2b[h, a, q] + s2a[h, a, 1 - q]
            i = (h, a)
            go(x2.at[h, a, :, pl.ds(2 - 2 * zl, 2)], zbuf.at[i], zs.at[i], zr.at[i], z_side)

    def scatter_end(h):
        for a in range(2):
            i = (h, a)
            arrived(zbuf.at[i], zs.at[i], zr.at[i])
            for q in range(2):
                rows = slice(a * 64 + q * 32, a * 64 + q * 32 + 32)
                agg[h, :, rows, :] = x2[h, a, q, pl.ds(2 * zl, 2)] + zbuf[h, a, q]

    def weight_start(h):
        turned = dot(agg[h, 0], feat_ref[:128]) + dot(agg[h, 1], feat_ref[128:])
        local[h] = turned.T.reshape(32, 8, 128)

        @pl.loop(1, 32)
        def _(j):
            to = (me + j) % 32
            copy_to(local.at[h, to], a1.at[h, me], w1s.at[h], w1r.at[h], plane(to)).start()

        a1[h, me] = local[h, me]

    def taken(buffer, sem, h):
        count = buffer.shape[1] - 1
        ref = buffer.at[h, pl.ds(0, count)]
        pltpu.make_async_copy(ref, ref, sem.at[h]).wait()

    def weight_sum(h):
        taken(a1, w1r, h)
        part[h] = jnp.sum(a1[h], axis=0)

        @pl.loop(1, 8)
        def _(j):
            copy_to(part.at[h], a2.at[h, mz], w2s.at[h], w2r.at[h], column((mz + j) % 8)).start()

        a2[h, mz] = part[h]

    def weight_spread(h):
        taken(a2, w2r, h)
        mine = gw_ref.at[pl.ds(me * 8, 8), pl.ds(h * 128, 128)]
        mine[...] = jnp.sum(a2[h], axis=0) * (1.0 / math.sqrt(65536))

        @pl.loop(1, 32)
        def _(j):
            copy_to(mine, mine, w3s.at[h], w3r.at[h], plane((me + j) % 32)).start()

    def weight_end(h):
        taken(a1, w3r, h)

    def step(name, *calls):
        with jax.named_scope(name):
            for call, *args in calls:
                call(*args)

    def clear():
        runs[0] = jnp.zeros((128, 128), F32)

    def wait_loads():
        for copy in loads:
            copy.wait()

    def features_gradient():
        for t in range(2):
            turned = dot(weight_ref[:, :128], agg[0, t]) + dot(weight_ref[:, 128:], agg[1, t])
            gf_ref[t * 128:(t + 1) * 128, :] = turned.T

    def wait_sends():
        for copy in started:
            copy.wait_send()
        for h in range(2):
            taken(a1, w1s, h)
            taken(a2, w2s, h)
            taken(a1, w3s, h)

    step("gather_own_0", (gather_own, 0))
    step("sort_tiles", (sort_tiles,), (clear,))
    step("gather_next_0", (gather_next, 0))
    step("gather_own_1", (gather_own, 1), (wait_loads,))
    step("gather_last_0", (gather_last, 0))
    step("products_0", (products, 0))
    step("scatter_start_0", (scatter_start, 0), (scatter_direct, 0))
    step("gather_next_1", (gather_next, 1))
    step("gather_last_1", (gather_last, 1))
    step("products_1", (products, 1))
    step("scatter_ring_0", (scatter_ring, 0))
    step("scatter_start_1", (scatter_start, 1), (scatter_direct, 1))
    for p in range(4):
        step("scatter_cross_0_%d" % p, (scatter_cross, 0, p))
    step("scatter_cross_ring_0", (scatter_cross_ring, 0))
    step("scatter_ring_1", (scatter_ring, 1))
    step("scatter_z_0", (scatter_z, 0))
    step("scatter_end_0", (scatter_end, 0))
    step("weight_start_0", (weight_start, 0))
    for p in range(3):
        step("scatter_cross_1_%d" % p, (scatter_cross, 1, p))
    step("weight_sum_0", (weight_sum, 0))
    step("scatter_cross_ring_1", (scatter_cross_ring, 1))
    step("scatter_cross_1_3", (scatter_cross, 1, 3))
    step("weight_spread_0", (weight_spread, 0))
    step("scatter_z_1", (scatter_z, 1))
    step("scatter_end_1", (scatter_end, 1))
    step("weight_start_1", (weight_start, 1))
    step("features_gradient", (weight_end, 0), (features_gradient,))
    step("weight_sum_1", (weight_sum, 1))
    step("weight_spread_1", (weight_spread, 1))
    step("weight_end_1", (weight_end, 1))
    step("wait_sends", (wait_sends,))


def on_device(features, pre_act, upstream, weight, tile_vals, tile_row, tile_col, tile_count):
    dma = pltpu.SemaphoreType.DMA
    square = jax.ShapeDtypeStruct((256, 256), F32)
    piece = (4, 32, 128)
    vmem = pl.BlockSpec(memory_space=pltpu.VMEM)
    return pl.pallas_call(
        kernel,
        out_shape=(square, square),
        in_specs=[vmem] * 6
        + [pl.BlockSpec(memory_space=pltpu.SMEM), pl.BlockSpec(memory_space=pl.ANY)],
        out_specs=(vmem, vmem),
        scratch_shapes=[
            pltpu.VMEM((SLOTS, 128, 128), F32),
            pltpu.VMEM((SLOTS + 1, 128, 128), F32),
            pltpu.VMEM((16, 128, 256), BF16),
            pltpu.VMEM((2, 16, 128, 128), F32),
            pltpu.VMEM((2, 4, 4, 4, 128, 128), F32),
            pltpu.VMEM((2, 2, 2, 4) + piece, F32),
            pltpu.VMEM((2, 2, 2, 4) + piece, F32),
            pltpu.VMEM((2, 2, 2, 4) + piece, F32),
            pltpu.VMEM((2, 2, 4, 2) + piece, F32),
            pltpu.VMEM((2, 2, 2) + piece, F32),
            pltpu.VMEM((2, 2, 2) + piece, F32),
            pltpu.VMEM((2, 2, 2) + piece, F32),
            pltpu.VMEM((2, 2, 2) + piece, F32),
            pltpu.VMEM((2, 2, 2, 2, 32, 128), F32),
            pltpu.VMEM((2, 2, 128, 128), F32),
            pltpu.VMEM((2, 32, 8, 128), F32),
            pltpu.VMEM((2, 32, 8, 128), F32),
            pltpu.VMEM((2, 8, 128), F32),
            pltpu.VMEM((2, 8, 8, 128), F32),
            pltpu.VMEM((8, 256), jnp.int32),
            pltpu.VMEM((8, 256), jnp.int32),
            pltpu.SMEM((8, 256), jnp.int32),
            dma((LOADS,)),
            dma,
            dma((2, 14)),
            dma((2, 14)),
        ]
        + [dma((2, 2, 2, 4))] * 6
        + [dma((2, 2, 2))] * 6
        + [dma((2, 2))] * 2
        + [dma((2,))] * 6,
        compiler_params=pltpu.CompilerParams(
            collective_id=0, has_side_effects=True, vmem_limit_bytes=56 << 20
        ),
        name="layer",
    )(
        pre_act, upstream, features, weight,
        tile_row.reshape(1, SLOTS), tile_col.reshape(1, SLOTS), tile_count, tile_vals,
    )


def solution(mesh):
    return jax.shard_map(
        on_device,
        mesh=mesh,
        in_specs=(
            P(("row", "col"), None),
            P(("row", "col"), None),
            P(("row", "col"), None),
            P(),
            P(("row", "col"), None, None),
            P(("row", "col")),
            P(("row", "col")),
            P(("row", "col")),
        ),
        out_specs=(P(("row", "col"), None), P()),
        check_vma=False,
    )
```

```python
import math

import jax
import jax.numpy as jnp
from jax import lax
from jax.experimental import pallas as pl
from jax.experimental.pallas import tpu as pltpu
from jax.sharding import PartitionSpec as P

MESH = pl.DeviceIdType.MESH
HIGH = lax.Precision.HIGHEST
F32 = jnp.float32
BF16 = jnp.bfloat16
SLOTS = 170
UNROLL = 34
LOADS = 10


def place():
    row = lax.axis_index("row")
    col = lax.axis_index("col")
    return row // 8, (row // 2) % 4, row % 2, col // 2, col % 2


def device(x, y, zl, zh, core):
    return (x * 8 + y * 2 + zl, zh * 2 + core)


def copy_to(src, dst, send, recv, target):
    return pltpu.make_async_remote_copy(
        src_ref=src, dst_ref=dst, send_sem=send, recv_sem=recv, device_id=target, device_id_type=MESH
    )


def split(value):
    high = value.astype(BF16)
    return high, (value - high.astype(F32)).astype(BF16)


def dot(a, b):
    return jnp.dot(a, b, precision=HIGH, preferred_element_type=F32)


def kernel(
    pre_ref, up_ref, feat_ref, weight_ref, row_ref, col_ref, count_ref, tiles_hbm,
    gf_ref, gw_ref,
    tiles, runs, parts, gt, sums, r1, r2a, r2b, x1, s1, s2a, s2b, x2, zbuf, fz, agg, local, a1, part, a2,
    raw, table_v, table,
    load_sem, table_sem, fzs, fzr, ag_s, ag_r, r1s, r1r, r2as, r2ar, r2bs, r2br, s1s, s1r, s2as, s2ar, s2bs, s2br, zs, zr,
    w1s, w1r, w2s, w2r, w3s, w3r,
):
    x, y, zl, zh, core = place()
    me = x * 8 + y * 2 + core
    mz = zh * 2 + zl
    here = zh * 4 + core * 2

    xs, ys, zhs = ([(v + d) % 4 for d in range(4)] for v in (x, y, zh))
    cores, zls = (core, 1 - core), (zl, 1 - zl)
    near = sorted(
        ((dx, dy, dc) for dx in range(4) for dy in range(4) for dc in range(2)),
        key=lambda d: -(d[0] % 2 + d[0] // 2 * 2 - d[0] // 3 * 2 + d[1] % 2 + d[1] // 2 * 2 - d[1] // 3 * 2),
    )
    plane = [
        (xs[dx] * 8 + ys[dy] * 2 + cores[dc], device(xs[dx], ys[dy], zl, zh, cores[dc]))
        for dx, dy, dc in near
        if (dx, dy, dc) != (0, 0, 0)
    ]
    column = [
        device(x, y, zls[dl], zhs[dh], core) for dh in (2, 1, 3, 0) for dl in (1, 0) if (dh, dl) != (0, 0)
    ]

    barrier = pltpu.get_barrier_semaphore()
    for peer in column + [peer for _, peer in plane]:
        pl.semaphore_signal(barrier, inc=1, device_id=peer, device_id_type=MESH)

    per_load = SLOTS // LOADS
    loads = []
    for i in range(LOADS):
        rows = pl.ds(i * per_load, per_load)
        loads.append(pltpu.make_async_copy(tiles_hbm.at[rows], tiles.at[rows], load_sem.at[i]))
        loads[-1].start()

    pre = pre_ref[...]
    gate = jax.nn.sigmoid(pre)
    grad = up_ref[...] * gate * (1.0 + pre * (1.0 - gate))
    for t in range(2):
        turned = grad[t * 128:(t + 1) * 128, :].T
        for h in range(2):
            gt[h, here + t] = turned[h * 128:(h + 1) * 128]
    pl.semaphore_wait(barrier, 38)

    started = []

    def go(src, dst, send, recv, target):
        copy = copy_to(src, dst, send, recv, target)
        copy.start()
        started.append(copy)

    z_right = device(x, y, zl, (zh + 1) % 4, core)
    z_left = device(x, y, zl, (zh + 3) % 4, core)
    sibling = device(x, y, zl, zh, 1 - core)
    z_side = device(x, y, 1 - zl, zh, core)
    x_side = (device((x + 1) % 4, y, zl, zh, core), device((x + 3) % 4, y, zl, zh, core))
    y_side = (device(x, (y + 1) % 4, zl, zh, core), device(x, (y + 3) % 4, zl, zh, core))

    def arrived(dst, send, recv):
        copy_to(dst, dst, send, recv, z_side).wait_recv()

    after, before, far = (zh + 1) % 4, (zh + 3) % 4, (zh + 2) % 4

    def block(h, block_zh, block_core, quarter):
        return gt.at[h, pl.ds(block_zh * 4 + block_core * 2, 2), pl.ds(quarter * 64, 64), :]

    def pass_on(h, block_zh, quarter, slot, target):
        ref = block(h, block_zh, core, quarter)
        go(ref, ref, ag_s.at[h, slot], ag_r.at[h, slot], target)

    def came(h, block_zh, block_core, quarter, slot):
        arrived(block(h, block_zh, block_core, quarter), ag_s.at[h, slot], ag_r.at[h, slot])

    def gather_own(h):
        pass_on(h, zh, 0, 0, z_right)
        pass_on(h, zh, 1, 3, z_left)
        pass_on(h, zh, 1, 1, z_right)
        pass_on(h, zh, 0, 2, z_left)
        pass_on(h, zh, 0, 6, sibling)
        pass_on(h, zh, 1, 7, sibling)

    def gather_next(h):
        came(h, before, core, 0, 0)
        pass_on(h, before, 0, 4, z_right)
        came(h, after, core, 1, 3)
        pass_on(h, after, 1, 5, z_left)
        pass_on(h, before, 0, 8, sibling)
        pass_on(h, after, 1, 9, sibling)
        came(h, before, core, 1, 1)
        pass_on(h, before, 1, 10, sibling)
        came(h, after, core, 0, 2)
        pass_on(h, after, 0, 11, sibling)

    def gather_last(h):
        came(h, far, core, 0, 4)
        pass_on(h, far, 0, 12, sibling)
        came(h, far, core, 1, 5)
        pass_on(h, far, 1, 13, sibling)
        blocks = ((zh, 0), (zh, 1), (before, 0), (after, 1), (before, 1), (after, 0), (far, 0), (far, 1))
        for i, (block_zh, quarter) in enumerate(blocks):
            came(h, block_zh, 1 - core, quarter, 6 + i)

    def sort_tiles():
        raw[...] = jnp.zeros((8, 256), jnp.int32)
        raw[0:1, 0:SLOTS] = col_ref[...]
        raw[1:2, 0:SLOTS] = row_ref[...]
        lane = lax.broadcasted_iota(jnp.int32, (8, 256), 1)
        across = lax.broadcasted_iota(jnp.int32, (256, 256), 1)
        slot_down = lax.broadcasted_iota(jnp.int32, (256, 1), 0)
        one, none = jnp.int32(1), jnp.int32(0)

        def down(value):
            return jnp.broadcast_to(value, (8, 256)).T[:, 0:1]

        def total(value):
            return jnp.sum(value, axis=0, keepdims=True)

        def within(value, last):
            return jnp.minimum(jnp.maximum(value, 0), last)

        values = raw[...]
        cols = jnp.where(lane < count_ref[...], values[0:1], 64)
        key = cols * 256 + lane
        rank = down(total(jnp.where(down(key[0:1]) < key[0:1], one, none)))
        col_down, row_down = down(cols[0:1]), down(values[1:2])
        at = rank == across
        next_at = rank + 1 == across
        sorted_cols = total(jnp.where(at, col_down, 0))
        previous = total(jnp.where(next_at, col_down + 1, 0)) - 1
        table_v[0:1] = within(total(jnp.where(at, slot_down, 0)), SLOTS - 1)
        table_v[1:2] = within(total(jnp.where(at, row_down, 0)), 15)
        table_v[2:3] = jnp.where(sorted_cols == previous, one, none)
        table_v[3:4] = within(total(jnp.where(col_down <= across, one, none)), SLOTS)
        table_v[4:5] = jnp.where(total(jnp.where(col_down == across, one, none)) > 0, one, none)
        table_v[5:8] = jnp.zeros((3, 256), jnp.int32)
        copy = pltpu.make_async_copy(table_v, table, table_sem)
        copy.start()
        copy.wait()

    def products(h):
        @pl.loop(0, 16)
        def _(i):
            high, low = split(gt[h, i])
            parts[i, :, :128] = high
            parts[i, :, 128:] = low

        @pl.loop(0, SLOTS // UNROLL)
        def _(i):
            for j in range(UNROLL):
                k = i * UNROLL + j
                high, low = split(tiles[table[0, k]])
                both = jnp.concatenate([high, low], axis=1)
                both = jnp.concatenate([both, both], axis=0)
                product = jnp.dot(parts[table[1, k]], both, preferred_element_type=F32)
                carried = table[2, k].astype(F32) * runs[k]
                runs[k + 1] = carried + product[:, :128] + product[:, 128:]

        @pl.loop(0, 16)
        def _(i):
            for j in range(4):
                t = i * 4 + j
                sums[h, i // 4, i % 4, j] = table[4, t].astype(F32) * runs[table[3, t]]

    first, second = (x_side, y_side), (y_side, x_side)
    c1, c2 = (x, y), (y, x)
    order = (2, 1, 3, 0)
    ahead = (1, 3)
    sides = tuple((a, d) for a in range(2) for d in range(2))

    def piece(h, a, d1, p, q):
        d1 = (c1[a] + d1) % 4
        d2 = (c2[a] + order[p]) % 4
        rows = pl.ds(a * 64 + q * 32, 32)
        return sums.at[h, d1, d2, :, rows, :] if a == 0 else sums.at[h, d2, d1, :, rows, :]

    def scatter_start(h):
        for p in range(4):
            for a, d in sides:
                i = (h, a, d, p)
                go(piece(h, a, 2, p, d), r1.at[i], r1s.at[i], r1r.at[i], first[a][d])

    def scatter_direct(h):
        for p in range(4):
            for a, d in sides:
                i = (h, a, d, p)
                go(piece(h, a, ahead[d], p, 1 - d), r2a.at[i], r2as.at[i], r2ar.at[i], first[a][d])

    def scatter_ring(h):
        for p in range(4):
            for a, d in sides:
                i = (h, a, d, p)
                arrived(r1.at[i], r1s.at[i], r1r.at[i])
                r1[i] += piece(h, a, ahead[d], p, d)[...]
                go(r1.at[i], r2b.at[i], r2bs.at[i], r2br.at[i], first[a][d])

    def scatter_cross(h, p):
        for a in range(2):
            for d in range(2):
                i = (h, a, d, p)
                arrived(r2a.at[i], r2as.at[i], r2ar.at[i])
                arrived(r2b.at[i], r2bs.at[i], r2br.at[i])
            for q in range(2):
                x1[h, a, p, q] = piece(h, a, 0, p, q)[...] + r2b[h, a, q, p] + r2a[h, a, 1 - q, p]
            if p == 0:
                for d in range(2):
                    i = (h, a, d)
                    go(x1.at[h, a, 0, d], s1.at[i], s1s.at[i], s1r.at[i], second[a][d])
            elif p < 3:
                i = (h, a, p - 1)
                go(x1.at[h, a, p, 2 - p], s2a.at[i], s2as.at[i], s2ar.at[i], second[a][p - 1])

    def scatter_cross_ring(h):
        for p in (1, 2):
            for a in range(2):
                i = (h, a, p - 1)
                arrived(s1.at[i], s1s.at[i], s1r.at[i])
                x1[h, a, p, p - 1] += s1[i]
                go(x1.at[h, a, p, p - 1], s2b.at[i], s2bs.at[i], s2br.at[i], second[a][p - 1])

    def scatter_z(h):
        for a in range(2):
            for d in range(2):
                i = (h, a, d)
                arrived(s2a.at[i], s2as.at[i], s2ar.at[i])
                arrived(s2b.at[i], s2bs.at[i], s2br.at[i])
            for q in range(2):
                rows = slice(a * 64 + q * 32, a * 64 + q * 32 + 32)
                x2[h, :, rows, :] = x1[h, a, 3, q] + s2b[h, a, q] + s2a[h, a, 1 - q]
            i = (h, a)
            rows = pl.ds(a * 64, 64)
            go(x2.at[h, pl.ds(2 - 2 * zl, 2), rows, :], zbuf.at[h, :, rows, :], zs.at[i], zr.at[i], z_side)

    def scatter_end(h):
        for a in range(2):
            i = (h, a)
            arrived(zbuf.at[h, :, pl.ds(a * 64, 64), :], zs.at[i], zr.at[i])
        agg[h] = x2[h, pl.ds(2 * zl, 2)] + zbuf[h]

    def features_send():
        go(feat_ref, fz, fzs, fzr, z_side)

    def features_wait():
        arrived(fz, fzs, fzr)

    def weight_start(h):
        turned = dot(x2[h, 2 * zl], feat_ref[:128]) + dot(x2[h, 2 * zl + 1], feat_ref[128:])
        turned += dot(x2[h, 2 - 2 * zl], fz[:128]) + dot(x2[h, 3 - 2 * zl], fz[128:])
        local[h] = turned.T.reshape(32, 8, 128)
        for to, peer in plane:
            copy_to(local.at[h, to], a1.at[h, me], w1s.at[h], w1r.at[h], peer).start()
        a1[h, me] = local[h, me]

    def taken(buffer, sem, h):
        count = buffer.shape[1] - 1
        ref = buffer.at[h, pl.ds(0, count)]
        pltpu.make_async_copy(ref, ref, sem.at[h]).wait()

    def weight_sum(h):
        taken(a1, w1r, h)
        part[h] = jnp.sum(a1[h], axis=0)
        for peer in column:
            copy_to(part.at[h], a2.at[h, mz], w2s.at[h], w2r.at[h], peer).start()
        a2[h, mz] = part[h]

    def weight_spread(h):
        taken(a2, w2r, h)
        mine = gw_ref.at[pl.ds(me * 8, 8), pl.ds(h * 128, 128)]
        mine[...] = jnp.sum(a2[h], axis=0) * (1.0 / math.sqrt(65536))
        for _, peer in plane:
            copy_to(mine, mine, w3s.at[h], w3r.at[h], peer).start()

    def weight_end(h):
        taken(a1, w3r, h)

    def step(name, *calls):
        with jax.named_scope(name):
            for call, *args in calls:
                call(*args)

    def clear():
        runs[0] = jnp.zeros((128, 128), F32)

    def wait_loads():
        for copy in loads:
            copy.wait()

    def features_gradient():
        for t in range(2):
            turned = dot(weight_ref[:, :128], agg[0, t]) + dot(weight_ref[:, 128:], agg[1, t])
            gf_ref[t * 128:(t + 1) * 128, :] = turned.T

    def wait_sends():
        for copy in started:
            copy.wait_send()
        for h in range(2):
            taken(a1, w1s, h)
            taken(a2, w2s, h)
            taken(a1, w3s, h)

    step("gather_own_0", (gather_own, 0))
    step("sort_tiles", (sort_tiles,), (clear,))
    step("gather_next_0", (gather_next, 0))
    step("gather_own_1", (gather_own, 1))
    step("loads", (wait_loads,))
    step("gather_last_0", (gather_last, 0))
    step("products_0", (products, 0))
    step("scatter_start_0", (scatter_start, 0), (scatter_direct, 0))
    step("gather_next_1", (gather_next, 1))
    step("gather_last_1", (gather_last, 1))
    step("weight_features_send", (features_send,))
    step("products_1", (products, 1))
    step("scatter_ring_0", (scatter_ring, 0))
    step("scatter_start_1", (scatter_start, 1), (scatter_direct, 1))
    for p in range(4):
        step("scatter_cross_0_%d" % p, (scatter_cross, 0, p))
    step("scatter_cross_ring_0", (scatter_cross_ring, 0))
    step("scatter_ring_1", (scatter_ring, 1))
    step("scatter_z_0", (scatter_z, 0))
    step("weight_start_0", (features_wait,), (weight_start, 0))
    for p in range(3):
        step("scatter_cross_1_%d" % p, (scatter_cross, 1, p))
    step("scatter_cross_ring_1", (scatter_cross_ring, 1))
    step("scatter_cross_1_3", (scatter_cross, 1, 3))
    step("weight_sum_0", (weight_sum, 0))
    step("scatter_z_1", (scatter_z, 1))
    step("weight_start_1", (weight_start, 1))
    step("weight_spread_0", (weight_spread, 0))
    step("scatter_end_0", (scatter_end, 0))
    step("scatter_end_1", (scatter_end, 1))
    step("features_gradient", (features_gradient,))
    step("weight_sum_1", (weight_sum, 1))
    step("weight_spread_1", (weight_spread, 1))
    step("weight_end_1", (weight_end, 0), (weight_end, 1))
    step("wait_sends", (wait_sends,))


def on_device(features, pre_act, upstream, weight, tile_vals, tile_row, tile_col, tile_count):
    dma = pltpu.SemaphoreType.DMA
    square = jax.ShapeDtypeStruct((256, 256), F32)
    piece = (4, 32, 128)
    vmem = pl.BlockSpec(memory_space=pltpu.VMEM)
    return pl.pallas_call(
        kernel,
        out_shape=(square, square),
        in_specs=[vmem] * 7 + [pl.BlockSpec(memory_space=pl.ANY)],
        out_specs=(vmem, vmem),
        scratch_shapes=[
            pltpu.VMEM((SLOTS, 128, 128), F32),
            pltpu.VMEM((SLOTS + 1, 128, 128), F32),
            pltpu.VMEM((16, 128, 256), BF16),
            pltpu.VMEM((2, 16, 128, 128), F32),
            pltpu.VMEM((2, 4, 4, 4, 128, 128), F32),
            pltpu.VMEM((2, 2, 2, 4) + piece, F32),
            pltpu.VMEM((2, 2, 2, 4) + piece, F32),
            pltpu.VMEM((2, 2, 2, 4) + piece, F32),
            pltpu.VMEM((2, 2, 4, 2) + piece, F32),
            pltpu.VMEM((2, 2, 2) + piece, F32),
            pltpu.VMEM((2, 2, 2) + piece, F32),
            pltpu.VMEM((2, 2, 2) + piece, F32),
            pltpu.VMEM((2, 4, 128, 128), F32),
            pltpu.VMEM((2, 2, 128, 128), F32),
            pltpu.VMEM((256, 256), F32),
            pltpu.VMEM((2, 2, 128, 128), F32),
            pltpu.VMEM((2, 32, 8, 128), F32),
            pltpu.VMEM((2, 32, 8, 128), F32),
            pltpu.VMEM((2, 8, 128), F32),
            pltpu.VMEM((2, 8, 8, 128), F32),
            pltpu.VMEM((8, 256), jnp.int32),
            pltpu.VMEM((8, 256), jnp.int32),
            pltpu.SMEM((8, 256), jnp.int32),
            dma((LOADS,)),
            dma,
            dma,
            dma,
            dma((2, 14)),
            dma((2, 14)),
        ]
        + [dma((2, 2, 2, 4))] * 6
        + [dma((2, 2, 2))] * 6
        + [dma((2, 2))] * 2
        + [dma((2,))] * 6,
        compiler_params=pltpu.CompilerParams(
            collective_id=0, has_side_effects=True, vmem_limit_bytes=48 << 20
        ),
        name="layer",
    )(
        pre_act, upstream, features, weight,
        tile_row.reshape(1, SLOTS), tile_col.reshape(1, SLOTS), tile_count.reshape(1, 1), tile_vals,
    )


def solution(mesh):
    return jax.shard_map(
        on_device,
        mesh=mesh,
        in_specs=(
            P(("row", "col"), None),
            P(("row", "col"), None),
            P(("row", "col"), None),
            P(),
            P(("row", "col"), None, None),
            P(("row", "col")),
            P(("row", "col")),
            P(("row", "col")),
        ),
        out_specs=(P(("row", "col"), None), P()),
        check_vma=False,
    )
```

```python
import math

import jax
import jax.numpy as jnp
from jax import lax
from jax.experimental import pallas as pl
from jax.experimental.pallas import tpu as pltpu
from jax.sharding import PartitionSpec as P

MESH = pl.DeviceIdType.MESH
HIGH = lax.Precision.HIGHEST
F32 = jnp.float32
BF16 = jnp.bfloat16
SLOTS = 170
UNROLL = 34
LOADS = 10


def place():
    row = lax.axis_index("row")
    col = lax.axis_index("col")
    return row // 8, (row // 2) % 4, row % 2, col // 2, col % 2


def device(x, y, zl, zh, core):
    return (x * 8 + y * 2 + zl, zh * 2 + core)


def copy_to(src, dst, send, recv, target):
    return pltpu.make_async_remote_copy(
        src_ref=src, dst_ref=dst, send_sem=send, recv_sem=recv, device_id=target, device_id_type=MESH
    )


def split(value):
    high = value.astype(BF16)
    return high, (value - high.astype(F32)).astype(BF16)


def dot(a, b):
    return jnp.dot(a, b, precision=HIGH, preferred_element_type=F32)


PARTS = ((0, 128), (128, 128))
SIDE = (48, 64)
REST = 32


def kernel(pre_hbm, up_hbm, feat_hbm, weight_hbm, row_hbm, col_hbm, count_hbm, tiles_hbm, gf_ref, gw_ref, ref, sem):
    x, y, zl, zh, core = place()
    me = x * 8 + y * 2 + core
    mz = zh * 2 + zl
    here = zh * 4 + core * 2

    loaded = {}

    def load(name, src, dst, slot):
        loaded[name] = pltpu.make_async_copy(src, dst, sem["in"].at[slot])
        loaded[name].start()

    load("pre", pre_hbm, ref["pre"], 0)
    load("up", up_hbm, ref["up"], 1)

    xs, ys, zhs = ([(v + d) % 4 for d in range(4)] for v in (x, y, zh))
    cores, zls = (core, 1 - core), (zl, 1 - zl)
    hops = (0, 1, 2, 1)
    offsets = [(dx, dy, dc) for dx in range(4) for dy in range(4) for dc in range(2) if dx + dy + dc]
    offsets.sort(key=lambda d: -hops[d[0]] - hops[d[1]])
    plane = [
        (xs[dx] * 8 + ys[dy] * 2 + cores[dc], device(xs[dx], ys[dy], zl, zh, cores[dc])) for dx, dy, dc in offsets
    ]
    column = [
        device(x, y, zls[dl], zhs[dh], core) for dh in (2, 1, 3, 0) for dl in (1, 0) if (dh, dl) != (0, 0)
    ]

    barrier = pltpu.get_barrier_semaphore()
    for peer in column + [peer for _, peer in plane]:
        pl.semaphore_signal(barrier, inc=1, device_id=peer, device_id_type=MESH)

    load("row", row_hbm, ref["row"], 2)
    load("col", col_hbm, ref["col"], 3)
    load("count", count_hbm, ref["count"], 4)
    per_load = SLOTS // LOADS
    for i in range(LOADS):
        rows = pl.ds(i * per_load, per_load)
        load(i, tiles_hbm.at[rows], ref["tiles"].at[rows], 7 + i)
    load("feat", feat_hbm, ref["feat"], 5)
    load("weight", weight_hbm, ref["weight"], 6)

    loaded["pre"].wait()
    loaded["up"].wait()
    pre = ref["pre"][...]
    gate = jax.nn.sigmoid(pre)
    grad = ref["up"][...] * gate * (1.0 + pre * (1.0 - gate))
    for t in range(2):
        turned = grad[t * 128:(t + 1) * 128, :].T
        for h, (low, size) in enumerate(PARTS):
            ref["gt"][h][here + t] = turned[low:low + size]
    pl.semaphore_wait(barrier, 38)

    started = []

    def go(src, dst, send, recv, target):
        copy = copy_to(src, dst, send, recv, target)
        copy.start()
        started.append(copy)

    z_right = device(x, y, zl, zhs[1], core)
    z_left = device(x, y, zl, zhs[3], core)
    sibling = device(x, y, zl, zh, 1 - core)
    z_side = device(x, y, 1 - zl, zh, core)
    x_side = (device(xs[1], y, zl, zh, core), device(xs[3], y, zl, zh, core))
    y_side = (device(x, ys[1], zl, zh, core), device(x, ys[3], zl, zh, core))

    def arrived(dst, send, recv):
        copy_to(dst, dst, send, recv, z_side).wait_recv()

    after, before, far = zhs[1], zhs[3], zhs[2]

    def block(h, block_zh, block_core, half):
        rows = PARTS[h][1] // 2
        return ref["gt"][h].at[pl.ds(block_zh * 4 + block_core * 2, 2), pl.ds(half * rows, rows), :]

    def pass_on(h, block_zh, half, slot, target):
        this = block(h, block_zh, core, half)
        go(this, this, sem["ag_s"].at[h, slot], sem["ag_r"].at[h, slot], target)

    def came(h, block_zh, block_core, half, slot):
        arrived(block(h, block_zh, block_core, half), sem["ag_s"].at[h, slot], sem["ag_r"].at[h, slot])

    def gather_own(h):
        pass_on(h, zh, 0, 0, z_right)
        pass_on(h, zh, 1, 3, z_left)
        pass_on(h, zh, 1, 1, z_right)
        pass_on(h, zh, 0, 2, z_left)
        pass_on(h, zh, 0, 6, sibling)
        pass_on(h, zh, 1, 7, sibling)

    def gather_next(h):
        came(h, before, core, 0, 0)
        pass_on(h, before, 0, 4, z_right)
        came(h, after, core, 1, 3)
        pass_on(h, after, 1, 5, z_left)
        pass_on(h, before, 0, 8, sibling)
        pass_on(h, after, 1, 9, sibling)

    def gather_rest(h):
        came(h, before, core, 1, 1)
        pass_on(h, before, 1, 10, sibling)
        came(h, after, core, 0, 2)
        pass_on(h, after, 0, 11, sibling)

    def gather_last(h):
        came(h, far, core, 0, 4)
        pass_on(h, far, 0, 12, sibling)
        came(h, far, core, 1, 5)
        pass_on(h, far, 1, 13, sibling)
        blocks = ((zh, 0), (zh, 1), (before, 0), (after, 1), (before, 1), (after, 0), (far, 0), (far, 1))
        for i, (block_zh, half) in enumerate(blocks):
            came(h, block_zh, 1 - core, half, 6 + i)

    def sort_tiles():
        raw, table_v = ref["raw"], ref["table_v"]
        for name in ("row", "col", "count"):
            loaded[name].wait()
        raw[...] = jnp.zeros((8, 256), jnp.int32)
        raw[0:1, 0:SLOTS] = ref["col"][...]
        raw[1:2, 0:SLOTS] = ref["row"][...]
        lane = lax.broadcasted_iota(jnp.int32, (8, 256), 1)
        across = lax.broadcasted_iota(jnp.int32, (256, 256), 1)
        slot_down = lax.broadcasted_iota(jnp.int32, (256, 1), 0)
        one, none = jnp.int32(1), jnp.int32(0)

        def down(value):
            return jnp.broadcast_to(value, (8, 256)).T[:, 0:1]

        def total(value):
            return jnp.sum(value, axis=0, keepdims=True)

        def within(value, last):
            return jnp.minimum(jnp.maximum(value, 0), last)

        values = raw[...]
        cols = jnp.where(lane < ref["count"][...], values[0:1], 64)
        key = cols * 256 + lane
        rank = down(total(jnp.where(down(key[0:1]) < key[0:1], one, none)))
        col_down, row_down = down(cols[0:1]), down(values[1:2])
        at = rank == across
        next_at = rank + 1 == across
        sorted_cols = total(jnp.where(at, col_down, 0))
        previous = total(jnp.where(next_at, col_down + 1, 0)) - 1
        table_v[0:1] = within(total(jnp.where(at, slot_down, 0)), SLOTS - 1)
        table_v[1:2] = within(total(jnp.where(at, row_down, 0)), 15)
        table_v[2:3] = jnp.where(sorted_cols == previous, one, none)
        table_v[3:4] = within(total(jnp.where(col_down <= across, one, none)), SLOTS)
        table_v[4:5] = jnp.where(total(jnp.where(col_down == across, one, none)) > 0, one, none)
        table_v[5:8] = jnp.zeros((3, 256), jnp.int32)
        copy = pltpu.make_async_copy(table_v, ref["table"], sem["table"])
        copy.start()
        copy.wait()
        ref["runs"][0] = jnp.zeros((128, 128), F32)

    def wait_tiles():
        for i in range(LOADS):
            loaded[i].wait()

    def split_part(h):
        size = PARTS[h][1]

        @pl.loop(0, 16)
        def _(i):
            high, low = split(ref["gt"][h][i])
            ref["bits"][i, :size, :128] = high
            ref["bits"][i, :size, 128:] = low

    def products(h, begin, end):
        size = PARTS[h][1]
        runs, table = ref["runs"], ref["table"]

        @pl.loop(begin, end)
        def _(i):
            for j in range(UNROLL):
                k = i * UNROLL + j
                high, low = split(ref["tiles"][table[0, k]])
                both = jnp.concatenate([high, low], axis=1)
                both = jnp.concatenate([both, both], axis=0)
                product = jnp.dot(ref["bits"][table[1, k], :size, :], both, preferred_element_type=F32)
                carried = table[2, k].astype(F32) * runs[k, :size, :]
                runs[k + 1, :size, :] = carried + product[:, :128] + product[:, 128:]

    def column_sums(h):
        size = PARTS[h][1]
        runs, table = ref["runs"], ref["table"]

        @pl.loop(0, 16)
        def _(i):
            for j in range(4):
                t = i * 4 + j
                ref["sums"][h][i // 4, i % 4, j] = table[4, t].astype(F32) * runs[table[3, t], :size, :]

    first, second = (x_side, y_side), (y_side, x_side)
    c1, c2 = (xs, ys), (ys, xs)
    order = (2, 1, 3, 0)
    ahead = (1, 3)
    sides = tuple((a, d) for a in range(2) for d in range(2))

    def piece(h, a, d1, p, q):
        quarter = SIDE[h] // 2
        d1, d2 = c1[a][d1], c2[a][order[p]]
        rows = pl.ds((a * 2 + q) * quarter, quarter)
        sums = ref["sums"][h]
        return sums.at[d1, d2, :, rows, :] if a == 0 else sums.at[d2, d1, :, rows, :]

    def sent(h, name, i, src, target):
        go(src, ref[name][h].at[i], sem[name + "s"].at[(h,) + i], sem[name + "r"].at[(h,) + i], target)

    def got(h, name, i):
        arrived(ref[name][h].at[i], sem[name + "s"].at[(h,) + i], sem[name + "r"].at[(h,) + i])
        return ref[name][h][i]

    def scatter_start(h):
        for p in range(4):
            for a, d in sides:
                sent(h, "r1", (a, d, p), piece(h, a, 2, p, d), first[a][d])

    def scatter_direct(h):
        for p in range(4):
            for a, d in sides:
                sent(h, "r2a", (a, d, p), piece(h, a, ahead[d], p, 1 - d), first[a][d])

    def scatter_ring(h):
        for p in range(4):
            for a, d in sides:
                i = (a, d, p)
                ref["r1"][h][i] = got(h, "r1", i) + piece(h, a, ahead[d], p, d)[...]
                sent(h, "r2b", i, ref["r1"][h].at[i], first[a][d])

    def scatter_cross(h, p):
        x1 = ref["x1"][h]
        for a in range(2):
            direct = [got(h, "r2a", (a, d, p)) for d in range(2)]
            around = [got(h, "r2b", (a, d, p)) for d in range(2)]
            for q in range(2):
                x1[a, p, q] = piece(h, a, 0, p, q)[...] + around[q] + direct[1 - q]
            if p == 0:
                for d in range(2):
                    sent(h, "s1", (a, d), x1.at[a, 0, d], second[a][d])
            elif p < 3:
                sent(h, "s2a", (a, p - 1), x1.at[a, p, 2 - p], second[a][p - 1])

    def scatter_cross_ring(h):
        x1 = ref["x1"][h]
        for p in (1, 2):
            for a in range(2):
                i = (a, p - 1)
                x1[a, p, p - 1] += got(h, "s1", i)
                sent(h, "s2b", i, x1.at[a, p, p - 1], second[a][p - 1])

    def z_refs(h, a, part):
        rows = pl.ds(a * SIDE[h], SIDE[h])
        return ref["x2"].at[h, pl.ds(part, 2), rows, :], ref["zbuf"].at[h, :, rows, :]

    def scatter_z(h):
        for a in range(2):
            direct = [got(h, "s2a", (a, d)) for d in range(2)]
            around = [got(h, "s2b", (a, d)) for d in range(2)]
            for q in range(2):
                rows = slice((2 * a + q) * SIDE[h] // 2, (2 * a + q + 1) * SIDE[h] // 2)
                ref["x2"][h, :, rows, :] = ref["x1"][h][a, 3, q] + around[q] + direct[1 - q]
            src, dst = z_refs(h, a, 2 - 2 * zl)
            go(src, dst, sem["zs"].at[h, a], sem["zr"].at[h, a], z_side)

    def scatter_end():
        for h in range(len(PARTS)):
            for a in range(2):
                arrived(z_refs(h, a, 0)[1], sem["zs"].at[h, a], sem["zr"].at[h, a])
        for g in range(2):
            ref["agg"][g] = ref["x2"][g, pl.ds(2 * zl, 2)] + ref["zbuf"][g]

    opposite = (device(x, ys[2], zl, zh, core), device(xs[2], y, zl, zh, core))

    def rest_send(h):
        for i in range(4):
            src = ref["sums"][h].at[i, :, pl.ds(2 - 2 * zl, 2), pl.ds(2 * SIDE[h], REST), :]
            sent(h, "rest", (i,), src, z_side)

    def rest_piece(h, a, d1, q):
        d1 = c1[a][d1]
        rows = pl.ds((a * 2 + q) * (REST // 4), REST // 4)
        rest = ref["rest"][h]
        return rest.at[d1, :, :, rows, :] if a == 0 else rest.at[:, d1, :, rows, :]

    def rest_start(h):
        for i in range(4):
            own = ref["sums"][h][i, :, pl.ds(2 * zl, 2), 2 * SIDE[h]:, :]
            ref["rest"][h][i] = got(h, "rest", (i,)) + own
        for a, d in sides:
            sent(h, "y1", (a, d), rest_piece(h, a, 2, d), first[a][d])
        for a, d in sides:
            sent(h, "y2a", (a, d), rest_piece(h, a, ahead[d], 1 - d), first[a][d])

    def rest_ring(h):
        for a, d in sides:
            ref["y1"][h][a, d] = got(h, "y1", (a, d)) + rest_piece(h, a, ahead[d], d)[...]
            sent(h, "y2b", (a, d), ref["y1"][h].at[a, d], first[a][d])

    def rest_cross(h):
        y3 = ref["y3"][h]
        for a in range(2):
            direct = [got(h, "y2a", (a, d)) for d in range(2)]
            around = [got(h, "y2b", (a, d)) for d in range(2)]
            for q in range(2):
                y3[a, q] = rest_piece(h, a, 0, q)[...] + around[q] + direct[1 - q]
            for p, target in enumerate((opposite[a], second[a][0], second[a][1])):
                sent(h, "y4", (a, p), y3.at[a, :, c2[a][order[p]]], target)

    def rest_end(h):
        for a in range(2):
            mine = ref["y3"][h][a, :, c2[a][0]]
            for p in range(3):
                mine += got(h, "y4", (a, p))
            for q in range(2):
                begin = 2 * SIDE[h] + (a * 2 + q) * (REST // 4)
                rows = slice(begin, begin + REST // 4)
                ref["x2"][h, pl.ds(2 * zl, 2), rows, :] = mine[q]
        none = jnp.zeros((2, REST, 128), F32)
        ref["x2"][h, pl.ds(2 - 2 * zl, 2), 2 * SIDE[h]:, :] = none
        ref["zbuf"][h, :, 2 * SIDE[h]:, :] = none

    def features_send():
        loaded["feat"].wait()
        go(ref["feat"], ref["fz"], sem["fzs"], sem["fzr"], z_side)

    def features_wait():
        arrived(ref["fz"], sem["fzs"], sem["fzr"])
        for name, zp in (("feat", zl), ("fz", 1 - zl)):
            rows = pl.ds(pl.multiple_of(zp * 256, 256), 256)
            ref["feat_high"][rows, :], ref["feat_low"][rows, :] = split(ref[name][...])

    def weight_start(g):
        x2, local = ref["x2"], ref["local"]
        high, low = split(jnp.concatenate([x2[g, i] for i in range(4)], axis=1))
        turned = sum(
            jnp.dot(a, ref[b][...], preferred_element_type=F32)
            for a, b in ((low, "feat_high"), (high, "feat_low"), (high, "feat_high"))
        )
        local[g] = turned.T.reshape(32, 8, 128)
        for to, peer in plane:
            copy_to(local.at[g, to], ref["a1"].at[g, me], sem["w1s"].at[g], sem["w1r"].at[g], peer).start()
        ref["a1"][g, me] = local[g, me]

    def taken(name, which, g):
        count = ref[name].shape[1] - 1
        some = ref[name].at[g, pl.ds(0, count)]
        pltpu.make_async_copy(some, some, sem[which].at[g]).wait()

    def weight_sum(g):
        taken("a1", "w1r", g)
        ref["part"][g] = jnp.sum(ref["a1"][g], axis=0)
        for peer in column:
            copy_to(ref["part"].at[g], ref["a2"].at[g, mz], sem["w2s"].at[g], sem["w2r"].at[g], peer).start()
        ref["a2"][g, mz] = ref["part"][g]

    def weight_spread(g):
        taken("a2", "w2r", g)
        mine = gw_ref.at[pl.ds(me * 8, 8), pl.ds(g * 128, 128)]
        mine[...] = jnp.sum(ref["a2"][g], axis=0) * (1.0 / math.sqrt(65536))
        for _, peer in plane:
            copy_to(mine, mine, sem["w3s"].at[g], sem["w3r"].at[g], peer).start()

    def weight_end():
        for g in range(2):
            taken("a1", "w3r", g)

    def features_gradient():
        agg, weight = ref["agg"], ref["weight"]
        loaded["weight"].wait()
        for t in range(2):
            turned = dot(weight[:, :128], agg[0, t]) + dot(weight[:, 128:], agg[1, t])
            gf_ref[t * 128:(t + 1) * 128, :] = turned.T

    def wait_sends():
        for copy in started:
            copy.wait_send()
        for g in range(2):
            taken("a1", "w1s", g)
            taken("a2", "w2s", g)
            taken("a1", "w3s", g)

    def cross(h, *places):
        for p in places:
            scatter_cross(h, p)

    chunks = SLOTS // UNROLL
    gather_own(0)
    sort_tiles()
    gather_next(0)
    gather_own(1)
    gather_rest(0)
    wait_tiles()
    gather_last(0)
    split_part(0)
    products(0, 0, 3)
    gather_next(1)
    products(0, 3, chunks)
    column_sums(0)
    scatter_start(0)
    scatter_direct(0)
    gather_rest(1)
    gather_last(1)
    rest_send(0)
    split_part(1)
    products(1, 0, 1)
    scatter_ring(0)
    products(1, 1, chunks)
    cross(0, 0, 1)
    column_sums(1)
    scatter_start(1)
    scatter_direct(1)
    features_send()
    cross(0, 2, 3)
    scatter_cross_ring(0)
    rest_start(0)
    scatter_ring(1)
    scatter_z(0)
    rest_ring(0)
    features_wait()
    cross(1, 0, 1)
    rest_cross(0)
    cross(1, 2)
    scatter_cross_ring(1)
    rest_end(0)
    weight_start(0)
    cross(1, 3)
    scatter_z(1)
    weight_start(1)
    weight_sum(0)
    scatter_end()
    features_gradient()
    weight_sum(1)
    weight_spread(0)
    weight_spread(1)
    weight_end()
    wait_sends()


def deliver(gf_ref, gw_ref, gf_out, gw_out):
    gf_out[...] = gf_ref[...]
    gw_out[...] = gw_ref[...]


def on_device(features, pre_act, upstream, weight, tile_vals, tile_row, tile_col, tile_count):
    dma = pltpu.SemaphoreType.DMA
    square = jax.ShapeDtypeStruct((256, 256), F32)
    count = len(PARTS)

    def f32(*shape):
        return pltpu.VMEM(shape, F32)

    def i32(*shape):
        return pltpu.VMEM(shape, jnp.int32)

    def pieces(*lead):
        return [f32(*lead, 4, side // 2, 128) for side in SIDE]

    def rests(*lead):
        return [f32(*lead, REST // 4, 128)]

    ref = dict(
        pre=f32(256, 256), up=f32(256, 256), feat=f32(256, 256), weight=f32(256, 256), fz=f32(256, 256),
        row=i32(1, SLOTS), col=i32(1, SLOTS), count=i32(1, 1), raw=i32(8, 256), table_v=i32(8, 256),
        table=pltpu.SMEM((8, 256), jnp.int32),
        tiles=f32(SLOTS, 128, 128),
        runs=f32(SLOTS + 1, 128, 128),
        bits=pltpu.VMEM((16, 128, 256), BF16),
        gt=[f32(16, size, 128) for _, size in PARTS],
        sums=[f32(4, 4, 4, size, 128) for _, size in PARTS],
        r1=pieces(2, 2, 4), r2a=pieces(2, 2, 4), r2b=pieces(2, 2, 4), x1=pieces(2, 4, 2),
        s1=pieces(2, 2), s2a=pieces(2, 2), s2b=pieces(2, 2),
        rest=[f32(4, 4, 2, REST, 128)],
        y1=rests(2, 2, 4, 2), y2a=rests(2, 2, 4, 2), y2b=rests(2, 2, 4, 2), y3=rests(2, 2, 4, 2), y4=rests(2, 3, 2, 2),
        feat_high=pltpu.VMEM((512, 256), BF16), feat_low=pltpu.VMEM((512, 256), BF16),
        x2=f32(2, 4, 128, 128), zbuf=f32(2, 2, 128, 128), agg=f32(2, 2, 128, 128),
        local=f32(2, 32, 8, 128), a1=f32(2, 32, 8, 128), part=f32(2, 8, 128), a2=f32(2, 8, 8, 128),
    )
    sem = {"in": dma((7 + LOADS,)), "table": dma, "fzs": dma, "fzr": dma}
    for side in "sr":
        sem["ag_" + side] = dma((count, 14))
        for name in ("r1", "r2a", "r2b"):
            sem[name + side] = dma((count, 2, 2, 4))
        for name in ("s1", "s2a", "s2b", "y1", "y2a", "y2b"):
            sem[name + side] = dma((count, 2, 2))
        sem["rest" + side] = dma((count, 4))
        sem["y4" + side] = dma((count, 2, 3))
        sem["z" + side] = dma((count, 2))
        for name in ("w1", "w2", "w3"):
            sem[name + side] = dma((2,))
    vmem = pl.BlockSpec(memory_space=pltpu.VMEM)
    hbm = pl.BlockSpec(memory_space=pltpu.HBM)
    results = pl.pallas_call(
        kernel,
        out_shape=(square, square),
        in_specs=[hbm] * 8,
        out_specs=(vmem, vmem),
        scratch_shapes=[ref, sem],
        compiler_params=pltpu.CompilerParams(
            collective_id=0, has_side_effects=True, vmem_limit_bytes=56 << 20
        ),
        name="layer",
    )(
        pre_act, upstream, features, weight,
        tile_row.reshape(1, SLOTS), tile_col.reshape(1, SLOTS), tile_count.reshape(1, 1), tile_vals,
    )
    return pl.pallas_call(
        deliver,
        out_shape=(square, square),
        in_specs=[vmem] * 2,
        out_specs=(vmem,) * 2,
        name="deliver",
    )(*results)


def solution(mesh):
    return jax.shard_map(
        on_device,
        mesh=mesh,
        in_specs=(
            P(("row", "col"), None),
            P(("row", "col"), None),
            P(("row", "col"), None),
            P(),
            P(("row", "col"), None, None),
            P(("row", "col")),
            P(("row", "col")),
            P(("row", "col")),
        ),
        out_specs=(P(("row", "col"), None), P()),
        check_vma=False,
    )
```

```python
import math

import jax
import jax.numpy as jnp
from jax import lax
from jax.experimental import pallas as pl
from jax.experimental.pallas import tpu as pltpu
from jax.sharding import PartitionSpec as P

MESH = pl.DeviceIdType.MESH
HIGH = lax.Precision.HIGHEST
F32 = jnp.float32
BF16 = jnp.bfloat16
SLOTS = 170
UNROLL = 34
LOADS = 10


def place():
    row = lax.axis_index("row")
    col = lax.axis_index("col")
    return row // 8, (row // 2) % 4, row % 2, col // 2, col % 2


def device(x, y, zl, zh, core):
    return (x * 8 + y * 2 + zl, zh * 2 + core)


def copy_to(src, dst, send, recv, target):
    return pltpu.make_async_remote_copy(
        src_ref=src, dst_ref=dst, send_sem=send, recv_sem=recv, device_id=target, device_id_type=MESH
    )


def split(value):
    high = value.astype(BF16)
    return high, (value - high.astype(F32)).astype(BF16)


def dot(a, b):
    return jnp.dot(a, b, precision=HIGH, preferred_element_type=F32)


PARTS = ((0, 128), (128, 128))
SIDE = (48, 64)
REST = 32


def kernel(pre_hbm, up_hbm, feat_hbm, weight_hbm, row_hbm, col_hbm, count_hbm, tiles_hbm, gf_ref, gw_ref, ref, sem):
    x, y, zl, zh, core = place()
    me = x * 8 + y * 2 + core
    mz = zh * 2 + zl
    here = zh * 4 + core * 2

    loaded = {}

    def load(name, src, dst, slot):
        loaded[name] = pltpu.make_async_copy(src, dst, sem["in"].at[slot])
        loaded[name].start()

    load("pre", pre_hbm, ref["pre"], 0)
    load("up", up_hbm, ref["up"], 1)

    xs, ys, zhs = ([(v + d) % 4 for d in range(4)] for v in (x, y, zh))
    cores, zls = (core, 1 - core), (zl, 1 - zl)
    hops = (0, 1, 2, 1)
    offsets = [(dx, dy, dc) for dx in range(4) for dy in range(4) for dc in range(2) if dx + dy + dc]
    offsets.sort(key=lambda d: -hops[d[0]] - hops[d[1]])
    plane = [
        (xs[dx] * 8 + ys[dy] * 2 + cores[dc], device(xs[dx], ys[dy], zl, zh, cores[dc])) for dx, dy, dc in offsets
    ]
    column = [
        device(x, y, zls[dl], zhs[dh], core) for dh in (2, 1, 3, 0) for dl in (1, 0) if (dh, dl) != (0, 0)
    ]

    barrier = pltpu.get_barrier_semaphore()
    for peer in column + [peer for _, peer in plane]:
        pl.semaphore_signal(barrier, inc=1, device_id=peer, device_id_type=MESH)

    load("row", row_hbm, ref["row"], 2)
    load("col", col_hbm, ref["col"], 3)
    load("count", count_hbm, ref["count"], 4)
    per_load = SLOTS // LOADS
    for i in range(LOADS):
        rows = pl.ds(i * per_load, per_load)
        load(i, tiles_hbm.at[rows], ref["tiles"].at[rows], 7 + i)
    load("feat", feat_hbm, ref["feat"], 5)
    load("weight", weight_hbm, ref["weight"], 6)

    loaded["pre"].wait()
    loaded["up"].wait()
    pre = ref["pre"][...]
    gate = jax.nn.sigmoid(pre)
    grad = ref["up"][...] * gate * (1.0 + pre * (1.0 - gate))
    for t in range(2):
        turned = grad[t * 128:(t + 1) * 128, :].T
        for h, (low, size) in enumerate(PARTS):
            ref["gt"][h][here + t] = turned[low:low + size]
    pl.semaphore_wait(barrier, 38)

    started = []

    def go(src, dst, send, recv, target):
        copy = copy_to(src, dst, send, recv, target)
        copy.start()
        started.append(copy)

    z_right = device(x, y, zl, zhs[1], core)
    z_left = device(x, y, zl, zhs[3], core)
    sibling = device(x, y, zl, zh, 1 - core)
    z_side = device(x, y, 1 - zl, zh, core)
    x_side = (device(xs[1], y, zl, zh, core), device(xs[3], y, zl, zh, core))
    y_side = (device(x, ys[1], zl, zh, core), device(x, ys[3], zl, zh, core))

    def arrived(dst, send, recv):
        copy_to(dst, dst, send, recv, z_side).wait_recv()

    after, before, far = zhs[1], zhs[3], zhs[2]

    def block(h, block_zh, block_core, half):
        rows = PARTS[h][1] // 2
        return ref["gt"][h].at[pl.ds(block_zh * 4 + block_core * 2, 2), pl.ds(half * rows, rows), :]

    def pass_on(h, block_zh, half, slot, target):
        this = block(h, block_zh, core, half)
        go(this, this, sem["ag_s"].at[h, slot], sem["ag_r"].at[h, slot], target)

    def came(h, block_zh, block_core, half, slot):
        arrived(block(h, block_zh, block_core, half), sem["ag_s"].at[h, slot], sem["ag_r"].at[h, slot])

    def gather_own(h):
        pass_on(h, zh, 0, 0, z_right)
        pass_on(h, zh, 1, 3, z_left)
        pass_on(h, zh, 1, 1, z_right)
        pass_on(h, zh, 0, 2, z_left)
        pass_on(h, zh, 0, 6, sibling)
        pass_on(h, zh, 1, 7, sibling)

    def gather_next(h):
        came(h, before, core, 0, 0)
        pass_on(h, before, 0, 4, z_right)
        came(h, after, core, 1, 3)
        pass_on(h, after, 1, 5, z_left)
        pass_on(h, before, 0, 8, sibling)
        pass_on(h, after, 1, 9, sibling)

    def gather_rest(h):
        came(h, before, core, 1, 1)
        pass_on(h, before, 1, 10, sibling)
        came(h, after, core, 0, 2)
        pass_on(h, after, 0, 11, sibling)

    def gather_last(h):
        came(h, far, core, 0, 4)
        pass_on(h, far, 0, 12, sibling)
        came(h, far, core, 1, 5)
        pass_on(h, far, 1, 13, sibling)
        blocks = ((zh, 0), (zh, 1), (before, 0), (after, 1), (before, 1), (after, 0), (far, 0), (far, 1))
        for i, (block_zh, half) in enumerate(blocks):
            came(h, block_zh, 1 - core, half, 6 + i)

    def sort_tiles():
        raw, table_v = ref["raw"], ref["table_v"]
        for name in ("row", "col", "count"):
            loaded[name].wait()
        raw[...] = jnp.zeros((8, 256), jnp.int32)
        raw[0:1, 0:SLOTS] = ref["col"][...]
        raw[1:2, 0:SLOTS] = ref["row"][...]
        lane = lax.broadcasted_iota(jnp.int32, (8, 256), 1)
        across = lax.broadcasted_iota(jnp.int32, (256, 256), 1)
        slot_down = lax.broadcasted_iota(jnp.int32, (256, 1), 0)
        one, none = jnp.int32(1), jnp.int32(0)

        def down(value):
            return jnp.broadcast_to(value, (8, 256)).T[:, 0:1]

        def total(value):
            return jnp.sum(value, axis=0, keepdims=True)

        def within(value, last):
            return jnp.minimum(jnp.maximum(value, 0), last)

        values = raw[...]
        cols = jnp.where(lane < ref["count"][...], values[0:1], 64)
        key = cols * 256 + lane
        rank = down(total(jnp.where(down(key[0:1]) < key[0:1], one, none)))
        col_down, row_down = down(cols[0:1]), down(values[1:2])
        at = rank == across
        next_at = rank + 1 == across
        sorted_cols = total(jnp.where(at, col_down, 0))
        previous = total(jnp.where(next_at, col_down + 1, 0)) - 1
        table_v[0:1] = within(total(jnp.where(at, slot_down, 0)), SLOTS - 1)
        table_v[1:2] = within(total(jnp.where(at, row_down, 0)), 15)
        table_v[2:3] = jnp.where(sorted_cols == previous, one, none)
        table_v[3:4] = within(total(jnp.where(col_down <= across, one, none)), SLOTS)
        table_v[4:5] = jnp.where(total(jnp.where(col_down == across, one, none)) > 0, one, none)
        table_v[5:8] = jnp.zeros((3, 256), jnp.int32)
        copy = pltpu.make_async_copy(table_v, ref["table"], sem["table"])
        copy.start()
        copy.wait()
        ref["runs"][0] = jnp.zeros((128, 128), F32)

    def wait_tiles():
        for i in range(LOADS):
            loaded[i].wait()

    def split_part(h):
        size = PARTS[h][1]

        @pl.loop(0, 16)
        def _(i):
            high, low = split(ref["gt"][h][i])
            ref["bits"][i, :size, :128] = high
            ref["bits"][i, :size, 128:] = low

    def products(h, begin, end):
        size = PARTS[h][1]
        runs, table = ref["runs"], ref["table"]

        @pl.loop(begin, end)
        def _(i):
            for j in range(UNROLL):
                k = i * UNROLL + j
                high, low = split(ref["tiles"][table[0, k]])
                both = jnp.concatenate([high, low], axis=1)
                both = jnp.concatenate([both, both], axis=0)
                product = jnp.dot(ref["bits"][table[1, k], :size, :], both, preferred_element_type=F32)
                carried = table[2, k].astype(F32) * runs[k, :size, :]
                runs[k + 1, :size, :] = carried + product[:, :128] + product[:, 128:]

    def column_sums(h):
        size = PARTS[h][1]
        runs, table = ref["runs"], ref["table"]

        @pl.loop(0, 16)
        def _(i):
            for j in range(4):
                t = i * 4 + j
                ref["sums"][h][i // 4, i % 4, j] = table[4, t].astype(F32) * runs[table[3, t], :size, :]

    first, second = (x_side, y_side), (y_side, x_side)
    c1, c2 = (xs, ys), (ys, xs)
    order = (2, 1, 3, 0)
    ahead = (1, 3)
    sides = tuple((a, d) for a in range(2) for d in range(2))

    def piece(h, a, d1, p, q):
        quarter = SIDE[h] // 2
        d1, d2 = c1[a][d1], c2[a][order[p]]
        rows = pl.ds((a * 2 + q) * quarter, quarter)
        sums = ref["sums"][h]
        return sums.at[d1, d2, :, rows, :] if a == 0 else sums.at[d2, d1, :, rows, :]

    def sent(h, name, i, src, target):
        go(src, ref[name][h].at[i], sem[name + "s"].at[(h,) + i], sem[name + "r"].at[(h,) + i], target)

    def got(h, name, i):
        arrived(ref[name][h].at[i], sem[name + "s"].at[(h,) + i], sem[name + "r"].at[(h,) + i])
        return ref[name][h][i]

    def scatter_start(h):
        for p in range(4):
            for a, d in sides:
                sent(h, "r1", (a, d, p), piece(h, a, 2, p, d), first[a][d])

    def scatter_direct(h):
        for p in range(4):
            for a, d in sides:
                sent(h, "r2a", (a, d, p), piece(h, a, ahead[d], p, 1 - d), first[a][d])

    def scatter_ring(h):
        for p in range(4):
            for a, d in sides:
                i = (a, d, p)
                ref["r1"][h][i] = got(h, "r1", i) + piece(h, a, ahead[d], p, d)[...]
                sent(h, "r2b", i, ref["r1"][h].at[i], first[a][d])

    def scatter_cross(h, p):
        x1 = ref["x1"][h]
        for a in range(2):
            direct = [got(h, "r2a", (a, d, p)) for d in range(2)]
            around = [got(h, "r2b", (a, d, p)) for d in range(2)]
            for q in range(2):
                x1[a, p, q] = piece(h, a, 0, p, q)[...] + around[q] + direct[1 - q]
            if p == 0:
                for d in range(2):
                    sent(h, "s1", (a, d), x1.at[a, 0, d], second[a][d])
            elif p < 3:
                sent(h, "s2a", (a, p - 1), x1.at[a, p, 2 - p], second[a][p - 1])

    def scatter_cross_ring(h):
        x1 = ref["x1"][h]
        for p in (1, 2):
            for a in range(2):
                i = (a, p - 1)
                x1[a, p, p - 1] += got(h, "s1", i)
                sent(h, "s2b", i, x1.at[a, p, p - 1], second[a][p - 1])

    def z_refs(h, a, part):
        rows = pl.ds(a * SIDE[h], SIDE[h])
        return ref["x2"].at[h, pl.ds(part, 2), rows, :], ref["zbuf"].at[h, :, rows, :]

    def scatter_z(h):
        for a in range(2):
            direct = [got(h, "s2a", (a, d)) for d in range(2)]
            around = [got(h, "s2b", (a, d)) for d in range(2)]
            for q in range(2):
                rows = slice((2 * a + q) * SIDE[h] // 2, (2 * a + q + 1) * SIDE[h] // 2)
                ref["x2"][h, :, rows, :] = ref["x1"][h][a, 3, q] + around[q] + direct[1 - q]
            src, dst = z_refs(h, a, 2 - 2 * zl)
            go(src, dst, sem["zs"].at[h, a], sem["zr"].at[h, a], z_side)

    def scatter_end():
        for h in range(len(PARTS)):
            for a in range(2):
                arrived(z_refs(h, a, 0)[1], sem["zs"].at[h, a], sem["zr"].at[h, a])
        for g in range(2):
            ref["agg"][g] = ref["x2"][g, pl.ds(2 * zl, 2)] + ref["zbuf"][g]

    opposite = (device(x, ys[2], zl, zh, core), device(xs[2], y, zl, zh, core))

    def rest_send(h):
        for i in range(4):
            src = ref["sums"][h].at[i, :, pl.ds(2 - 2 * zl, 2), pl.ds(2 * SIDE[h], REST), :]
            sent(h, "rest", (i,), src, z_side)

    def rest_piece(h, a, d1, q):
        d1 = c1[a][d1]
        rows = pl.ds((a * 2 + q) * (REST // 4), REST // 4)
        rest = ref["rest"][h]
        return rest.at[d1, :, :, rows, :] if a == 0 else rest.at[:, d1, :, rows, :]

    def rest_start(h):
        for i in range(4):
            own = ref["sums"][h][i, :, pl.ds(2 * zl, 2), 2 * SIDE[h]:, :]
            ref["rest"][h][i] = got(h, "rest", (i,)) + own
        for a, d in sides:
            sent(h, "y1", (a, d), rest_piece(h, a, 2, d), first[a][d])
        for a, d in sides:
            sent(h, "y2a", (a, d), rest_piece(h, a, ahead[d], 1 - d), first[a][d])

    def rest_ring(h):
        for a, d in sides:
            ref["y1"][h][a, d] = got(h, "y1", (a, d)) + rest_piece(h, a, ahead[d], d)[...]
            sent(h, "y2b", (a, d), ref["y1"][h].at[a, d], first[a][d])

    def rest_cross(h):
        y3 = ref["y3"][h]
        for a in range(2):
            direct = [got(h, "y2a", (a, d)) for d in range(2)]
            around = [got(h, "y2b", (a, d)) for d in range(2)]
            for q in range(2):
                y3[a, q] = rest_piece(h, a, 0, q)[...] + around[q] + direct[1 - q]
            for p, target in enumerate((opposite[a], second[a][0], second[a][1])):
                sent(h, "y4", (a, p), y3.at[a, :, c2[a][order[p]]], target)

    def rest_end(h):
        for a in range(2):
            mine = ref["y3"][h][a, :, c2[a][0]]
            for p in range(3):
                mine += got(h, "y4", (a, p))
            for q in range(2):
                begin = 2 * SIDE[h] + (a * 2 + q) * (REST // 4)
                rows = slice(begin, begin + REST // 4)
                ref["x2"][h, pl.ds(2 * zl, 2), rows, :] = mine[q]
        none = jnp.zeros((2, REST, 128), F32)
        ref["x2"][h, pl.ds(2 - 2 * zl, 2), 2 * SIDE[h]:, :] = none
        ref["zbuf"][h, :, 2 * SIDE[h]:, :] = none

    def features_send():
        loaded["feat"].wait()
        go(ref["feat"], ref["fz"], sem["fzs"], sem["fzr"], z_side)

    def features_wait():
        arrived(ref["fz"], sem["fzs"], sem["fzr"])
        for name, zp in (("feat", zl), ("fz", 1 - zl)):
            rows = pl.ds(pl.multiple_of(zp * 256, 256), 256)
            ref["feat_high"][rows, :], ref["feat_low"][rows, :] = split(ref[name][...])

    def weight_start(g):
        x2, local = ref["x2"], ref["local"]
        high, low = split(jnp.concatenate([x2[g, i] for i in range(4)], axis=1))
        turned = sum(
            jnp.dot(a, ref[b][...], preferred_element_type=F32)
            for a, b in ((low, "feat_high"), (high, "feat_low"), (high, "feat_high"))
        )
        local[g] = turned.T.reshape(32, 8, 128)
        for to, peer in plane:
            copy_to(local.at[g, to], ref["a1"].at[g, me], sem["w1s"].at[g], sem["w1r"].at[g], peer).start()
        ref["a1"][g, me] = local[g, me]

    def taken(name, which, g):
        count = ref[name].shape[1] - 1
        some = ref[name].at[g, pl.ds(0, count)]
        pltpu.make_async_copy(some, some, sem[which].at[g]).wait()

    def weight_sum(g):
        taken("a1", "w1r", g)
        ref["part"][g] = jnp.sum(ref["a1"][g], axis=0)
        for peer in column:
            copy_to(ref["part"].at[g], ref["a2"].at[g, mz], sem["w2s"].at[g], sem["w2r"].at[g], peer).start()
        ref["a2"][g, mz] = ref["part"][g]

    def weight_spread(g):
        taken("a2", "w2r", g)
        mine = gw_ref.at[pl.ds(me * 8, 8), pl.ds(g * 128, 128)]
        mine[...] = jnp.sum(ref["a2"][g], axis=0) * (1.0 / math.sqrt(65536))
        for _, peer in plane:
            copy_to(mine, mine, sem["w3s"].at[g], sem["w3r"].at[g], peer).start()

    def weight_end():
        for g in range(2):
            taken("a1", "w3r", g)

    def features_gradient():
        agg, weight = ref["agg"], ref["weight"]
        loaded["weight"].wait()
        for t in range(2):
            turned = dot(weight[:, :128], agg[0, t]) + dot(weight[:, 128:], agg[1, t])
            gf_ref[t * 128:(t + 1) * 128, :] = turned.T

    def wait_sends():
        for copy in started:
            copy.wait_send()
        for g in range(2):
            taken("a1", "w1s", g)
            taken("a2", "w2s", g)
            taken("a1", "w3s", g)

    def cross(h, *places):
        for p in places:
            scatter_cross(h, p)

    chunks = SLOTS // UNROLL
    gather_own(0)
    sort_tiles()
    gather_next(0)
    gather_own(1)
    gather_rest(0)
    wait_tiles()
    gather_last(0)
    split_part(0)
    products(0, 0, 3)
    gather_next(1)
    products(0, 3, chunks)
    column_sums(0)
    scatter_start(0)
    scatter_direct(0)
    gather_rest(1)
    gather_last(1)
    rest_send(0)
    split_part(1)
    products(1, 0, 1)
    scatter_ring(0)
    products(1, 1, chunks)
    cross(0, 0, 1)
    column_sums(1)
    scatter_start(1)
    scatter_direct(1)
    features_send()
    cross(0, 2, 3)
    scatter_cross_ring(0)
    scatter_ring(1)
    scatter_z(0)
    rest_start(0)
    cross(1, 0, 1)
    rest_ring(0)
    cross(1, 2)
    scatter_cross_ring(1)
    rest_cross(0)
    features_wait()
    rest_end(0)
    weight_start(0)
    cross(1, 3)
    scatter_z(1)
    weight_start(1)
    weight_sum(0)
    scatter_end()
    features_gradient()
    weight_sum(1)
    weight_spread(0)
    weight_spread(1)
    weight_end()
    wait_sends()


def on_device(features, pre_act, upstream, weight, tile_vals, tile_row, tile_col, tile_count):
    dma = pltpu.SemaphoreType.DMA
    count = len(PARTS)

    def f32(*shape):
        return pltpu.VMEM(shape, F32)

    def i32(*shape):
        return pltpu.VMEM(shape, jnp.int32)

    def pieces(*lead):
        return [f32(*lead, 4, side // 2, 128) for side in SIDE]

    def rests(*lead):
        return [f32(*lead, REST // 4, 128)]

    ref = dict(
        pre=f32(256, 256), up=f32(256, 256), feat=f32(256, 256), weight=f32(256, 256), fz=f32(256, 256),
        row=i32(1, SLOTS), col=i32(1, SLOTS), count=i32(1, 1), raw=i32(8, 256), table_v=i32(8, 256),
        table=pltpu.SMEM((8, 256), jnp.int32),
        tiles=f32(SLOTS, 128, 128),
        runs=f32(SLOTS + 1, 128, 128),
        bits=pltpu.VMEM((16, 128, 256), BF16),
        gt=[f32(16, size, 128) for _, size in PARTS],
        sums=[f32(4, 4, 4, size, 128) for _, size in PARTS],
        r1=pieces(2, 2, 4), r2a=pieces(2, 2, 4), r2b=pieces(2, 2, 4), x1=pieces(2, 4, 2),
        s1=pieces(2, 2), s2a=pieces(2, 2), s2b=pieces(2, 2),
        rest=[f32(4, 4, 2, REST, 128)],
        y1=rests(2, 2, 4, 2), y2a=rests(2, 2, 4, 2), y2b=rests(2, 2, 4, 2), y3=rests(2, 2, 4, 2), y4=rests(2, 3, 2, 2),
        feat_high=pltpu.VMEM((512, 256), BF16), feat_low=pltpu.VMEM((512, 256), BF16),
        x2=f32(2, 4, 128, 128), zbuf=f32(2, 2, 128, 128), agg=f32(2, 2, 128, 128),
        local=f32(2, 32, 8, 128), a1=f32(2, 32, 8, 128), part=f32(2, 8, 128), a2=f32(2, 8, 8, 128),
    )
    sem = {"in": dma((7 + LOADS,)), "table": dma, "fzs": dma, "fzr": dma}
    for side in "sr":
        sem["ag_" + side] = dma((count, 14))
        for name in ("r1", "r2a", "r2b"):
            sem[name + side] = dma((count, 2, 2, 4))
        for name in ("s1", "s2a", "s2b", "y1", "y2a", "y2b"):
            sem[name + side] = dma((count, 2, 2))
        sem["rest" + side] = dma((count, 4))
        sem["y4" + side] = dma((count, 2, 3))
        sem["z" + side] = dma((count, 2))
        for name in ("w1", "w2", "w3"):
            sem[name + side] = dma((2,))
    vmem = pl.BlockSpec(memory_space=pltpu.VMEM)
    hbm = pl.BlockSpec(memory_space=pltpu.HBM)
    return pl.pallas_call(
        kernel,
        out_shape=(f32(256, 256), f32(256, 256)),
        in_specs=[hbm] * 8,
        out_specs=(vmem, vmem),
        scratch_shapes=[ref, sem],
        compiler_params=pltpu.CompilerParams(
            collective_id=0, has_side_effects=True, vmem_limit_bytes=56 << 20
        ),
        name="layer",
    )(
        pre_act, upstream, features, weight,
        tile_row.reshape(1, SLOTS), tile_col.reshape(1, SLOTS), tile_count.reshape(1, 1), tile_vals,
    )


def solution(mesh):
    return jax.shard_map(
        on_device,
        mesh=mesh,
        in_specs=(
            P(("row", "col"), None),
            P(("row", "col"), None),
            P(("row", "col"), None),
            P(),
            P(("row", "col"), None, None),
            P(("row", "col")),
            P(("row", "col")),
            P(("row", "col")),
        ),
        out_specs=(P(("row", "col"), None), P()),
        check_vma=False,
    )
```
